128 devices in a mesh: segment: 2 (over y_lo), blk: 8 (over z, y_hi), rows: 8 (over x, core).
Axes of the slice: x: 4, y: 4 (y_hi: 2, y_lo: 2; y = y_hi * 2 + y_lo), z: 4, core: 2. Of those that a mesh axis runs over, the one named last changes fastest.
Arguments:
- nodal_disp: float32 [8, 3, 262144], P(None, None, ('blk', 'rows')), may hold values from -0.3 to 0.3
- connect: int32 [8, 262144], P(None, ('blk', 'rows')), may hold values from 0 to 4095
- brick_size: float32 [262144], P(('blk', 'rows')), may hold values from 0.5 to 2
- shear_modulus: float32 [262144], P(('blk', 'rows')), may hold values from 3 to 12
- bulk_modulus: float32 [262144], P(('blk', 'rows')), may hold values from 5 to 20
- cohesion: float32 [262144], P(('blk', 'rows')), may hold values from 0.3 to 3
- friction: float32 [262144], P(('blk', 'rows')), may hold values from 0.1 to 0.6
- active: int32 [262144], P(('blk', 'rows')), may hold values 0 or 1
- patch_brick: int32 [16384], P(('blk', 'rows')), may hold values from 0 to 4095
- patch_face: int32 [16384], P(('blk', 'rows')), may hold values from 0 to 5
- coords: float32 [3, 16384], P(None, ('blk', 'rows')), may hold values from -1 to 17, as said below
- radius: float32 [16384], P(('blk', 'rows')), may hold values from 0.03 to 0.0625
- stiffness: float32 [16384], P(('blk', 'rows')), may hold values from 0.1 to 0.3
Outputs:
- relaxed: float32 [8, 3, 16384], P(None, None, ('blk', 'rows'))
The draws below stay inside these ranges and needn't reach their ends.
Inputs may be any that keep to these rules, and one draw needn't show every extreme that they name: `connect`: indexes the mesh nodes of the brick's own block. `patch_brick`: indexes the bricks of the node's own block. `patch_face`: 2 k for the plus face along dimension k, 2 k + 1 for the minus face. `coords`: collocation points on the slab.
All inputs are finite; a program needn't handle non-finite values. No bound on the sum of `active` on one device may be relied on, other than what follows from the above.
Results may differ from the reference program's by a relative error of at most 0.0004.
The reference program's roundings to bfloat16 on the way count: a program that leaves them out, or rounds other values in their place, can miss the bound.
Values may be sent and summed in bfloat16 or wider, within the bound.
A program may use at most 192 MiB of HBM per device.

```python
import math
import jax
import jax.numpy as jnp
from jax import lax

BATCHES = 8
SWEEPS = 3
NODE_DEV = 256
BRICK_DEV = 4096
SLAB_NODES = 16384
BRICKS = 262144


def draw_coords(key, part):
    key = jax.random.fold_in(key, 11)
    place_key = jax.random.fold_in(key, 5)
    jitter_key = jax.random.fold_in(key, 7)
    position = jax.random.permutation(place_key, SLAB_NODES)
    column = (position % 128).astype(jnp.float32)
    grid_row = (position // 128).astype(jnp.float32)
    jitter = jax.random.uniform(jitter_key, (3, SLAB_NODES), jnp.float32, -1.0, 1.0)
    height = 0.2
    spacing = 0.0625
    first_axis = (column + 0.3 * jitter[0]) * spacing
    second_axis = (grid_row + 0.3 * jitter[1]) * spacing
    third_axis = height * jitter[2] * spacing
    return jnp.stack([first_axis, second_axis, third_axis])


def set_ends(values, rng, least, high):
    longest = values.shape.index(max(values.shape))
    spots = []
    for shift in (0, 1):
        where = [jax.random.randint(jax.random.fold_in(rng, axis), (), 0, length) for axis, length in enumerate(values.shape)]
        where[longest] = (where[longest] + shift) % values.shape[longest]
        spots.append(tuple(where))
    return values.at[spots[0]].set(least).at[spots[1]].set(high)


def level_of(key, extent, cuts, low, high):
    loudness = 1.0
    for dim, blocks in cuts:
        steps = jax.random.uniform(jax.random.fold_in(jax.random.fold_in(key, 6), dim), (blocks,), jnp.float32, low / len(cuts), high / len(cuts))
        loudness = loudness * jnp.repeat(jnp.exp(steps), extent[dim] // blocks).reshape((-1,) + (1,) * (len(extent) - 1 - dim))
    return loudness


def noise(own_key, extent, scale, limit, cuts=(), kind=jnp.bfloat16):
    level = level_of(own_key, extent, cuts, -0.22, 0.18) if cuts else 1.0
    values = jax.random.normal(own_key, extent, jnp.float32) * scale * level
    return jnp.minimum(jnp.maximum(values, -limit), limit).astype(kind)


def setup_inputs(seed: int = 0) -> dict:
    arg_keys = jax.random.split(jax.random.key(seed), 14)
    return {
        "nodal_disp": noise(arg_keys[0], (BATCHES, 3, BRICKS), 0.05, 0.3, ((2, 64),), jnp.float32),
        "connect": set_ends(jax.random.randint(arg_keys[1], (8, BRICKS), 0, BRICK_DEV), jax.random.fold_in(arg_keys[1], 1), 0, BRICK_DEV - 1).astype(jnp.int32),
        "brick_size": jnp.clip(jnp.exp(math.log(2.0) - 1.3862944 * jax.random.uniform(arg_keys[2], (BRICKS,), jnp.float32) ** level_of(arg_keys[2], (BRICKS,), ((0, 64),), -0.2, 0.2)), 0.5, 2.0),
        "shear_modulus": jnp.clip(jnp.exp(math.log(12.0) - 1.3862944 * jax.random.uniform(arg_keys[3], (BRICKS,), jnp.float32) ** level_of(arg_keys[3], (BRICKS,), ((0, 64),), -0.2, 0.2)), 3.0, 12.0),
        "bulk_modulus": jnp.clip(jnp.exp(math.log(20.0) - 1.3862944 * jax.random.uniform(arg_keys[4], (BRICKS,), jnp.float32) ** level_of(arg_keys[4], (BRICKS,), ((0, 64),), -0.2, 0.2)), 5.0, 20.0),
        "cohesion": jnp.clip(jnp.exp(math.log(3.0) - 2.3025851 * jax.random.uniform(arg_keys[5], (BRICKS,), jnp.float32) ** level_of(arg_keys[5], (BRICKS,), ((0, 64),), -0.2, 0.2)), 0.3, 3.0),
        "friction": jnp.clip(0.1 + 0.5 * jax.random.uniform(arg_keys[6], (BRICKS,), jnp.float32) ** level_of(arg_keys[6], (BRICKS,), ((0, 64),), -0.2, 0.2), 0.1, 0.6),
        "active": set_ends((jax.random.randint(arg_keys[7], (BRICKS,), 0, 2) < 1).astype(jnp.int32), jax.random.fold_in(arg_keys[7], 1), 0, 1),
        "patch_brick": set_ends(jax.random.randint(arg_keys[8], (SLAB_NODES,), 0, BRICK_DEV), jax.random.fold_in(arg_keys[8], 1), 0, BRICK_DEV - 1).astype(jnp.int32),
        "patch_face": set_ends(jax.random.randint(arg_keys[9], (SLAB_NODES,), 0, 6), jax.random.fold_in(arg_keys[9], 1), 0, 5).astype(jnp.int32),
        "coords": draw_coords(jax.random.fold_in(arg_keys[13], 71), 0),
        "radius": jnp.clip(jnp.exp(math.log(0.0625) - 0.7339692 * jax.random.uniform(arg_keys[11], (SLAB_NODES,), jnp.float32) ** level_of(arg_keys[11], (SLAB_NODES,), ((0, 64),), -0.2, 0.2)), 0.03, 0.0625),
        "stiffness": jnp.clip(jnp.exp(math.log(0.3) - 1.0986123 * jax.random.uniform(arg_keys[12], (SLAB_NODES,), jnp.float32) ** level_of(arg_keys[12], (SLAB_NODES,), ((0, 64),), -0.2, 0.2)), 0.1, 0.3),
    }


KELVIN_A = 1.0 / (1024.0 * math.pi)
KELVIN_B = KELVIN_A / 3.0
SMOOTH = 0.1
RELAXATION = 0.5

def corner_sign():
    corner = jnp.arange(8)
    powers = jnp.array([1, 2, 4])
    corner_bits = corner[:, None] // powers[None, :] % 2
    return (2 * corner_bits - 1).astype(jnp.float32)

def brick_stress(nodal_disp, connect, brick_size, shear_modulus, bulk_modulus, cohesion, friction, active):
    signs_table = corner_sign()
    gradient = jnp.zeros((nodal_disp.shape[0], 3, 3, connect.shape[1]), jnp.float32)
    centre = jnp.zeros((nodal_disp.shape[0], 3, connect.shape[1]), jnp.float32)
    for corner in range(8):
        corner_disp = jnp.take(nodal_disp, connect[corner], axis=2)
        gradient = gradient + corner_disp[:, :, None, :] * signs_table[corner][None, None, :, None]
        centre = centre + corner_disp
    gradient = gradient / (4.0 * brick_size)
    centre = centre / 8.0
    strain = 0.5 * (gradient + jnp.swapaxes(gradient, 1, 2))
    volume = strain[:, 0, 0] + strain[:, 1, 1] + strain[:, 2, 2]
    identity = jnp.eye(3, dtype=jnp.float32)[None, :, :, None]
    pressure = bulk_modulus * volume
    deviator = 2.0 * shear_modulus * (strain - volume[:, None, None, :] / 3.0 * identity)
    second = 0.5 * lax.optimization_barrier(jnp.sum(deviator * deviator, axis=(1, 2)))
    scaling = jnp.maximum(cohesion - friction * pressure, SMOOTH) / jnp.sqrt(second + SMOOTH * SMOOTH)
    scaling = jnp.where(active == 1, scaling, 1.0)
    stress = scaling[:, None, None, :] * deviator + pressure[:, None, None, :] * identity
    return (stress, centre)

def interface(stress, centre, patch_brick, patch_face):
    picked = jnp.take(stress, patch_brick, axis=3)
    axis_of = patch_face // 2
    sign_of = (1 - 2 * (patch_face % 2)).astype(jnp.float32)
    normal = (jnp.arange(3)[:, None] == axis_of[None, :]).astype(jnp.float32) * sign_of[None, :]
    traction = lax.optimization_barrier(jnp.sum(picked * normal[None, None, :, :], axis=2))
    fem_disp = jnp.take(centre, patch_brick, axis=2)
    return (traction.astype(jnp.bfloat16), fem_disp.astype(jnp.bfloat16))

def kelvin_tile(targets, points):
    offset = targets[:, :, None] - points[:3, None, :]
    spread = points[3]
    squared = lax.optimization_barrier(jnp.sum(offset * offset, axis=0)) + spread[None, :] * spread[None, :]
    inverse = lax.rsqrt(squared)
    inverse_cube = inverse * inverse * inverse
    diagonal = (KELVIN_A - KELVIN_B) * inverse + 0.5 * KELVIN_A * spread[None, :] * spread[None, :] * inverse_cube
    identity = jnp.eye(3, dtype=jnp.float32)[:, :, None, None]
    kernel_tile = identity * diagonal[None, None] + KELVIN_B * inverse_cube[None, None] * offset[:, None] * offset[None, :]
    return kernel_tile.astype(jnp.bfloat16)

def apply_kernel(points, density):
    node_count = points.shape[1]
    block_width = math.gcd(node_count, 128)
    targets = points[:3].reshape(3, node_count // block_width, block_width).transpose(1, 0, 2)
    density_wide = density.astype(jnp.float32)

    def per_block(target_block):
        kernel_tile = kelvin_tile(target_block, points)
        return jnp.einsum('mbk,abnk->man', density_wide, kernel_tile.astype(jnp.float32))
    result = lax.map(per_block, targets)
    return result.transpose(1, 2, 0, 3).reshape(density.shape[0], 3, node_count)

def reference(nodal_disp, connect, brick_size, shear_modulus, bulk_modulus, cohesion, friction, active, patch_brick, patch_face, coords, radius, stiffness):
    brick_block = (jnp.arange(BRICKS) // BRICK_DEV * BRICK_DEV).astype(jnp.int32)
    stress, centre = brick_stress(nodal_disp, connect + brick_block[None, :], brick_size, shear_modulus, bulk_modulus, cohesion, friction, active)
    node_block = (jnp.arange(SLAB_NODES) // NODE_DEV * BRICK_DEV).astype(jnp.int32)
    traction, fem_disp = interface(stress, centre, patch_brick + node_block, patch_face)
    points = jnp.concatenate([coords, radius[None, :]], axis=0)
    trac_wide = traction.astype(jnp.float32)
    displacement = apply_kernel(points, traction)
    for sweep_step in range(1, SWEEPS):
        density = (trac_wide - stiffness[None, None, :] * displacement).astype(jnp.bfloat16)
        displacement = apply_kernel(points, density)
    fem_wide = fem_disp.astype(jnp.float32)
    return fem_wide + RELAXATION * (displacement - fem_wide)
```

```python
import math

import jax
import jax.numpy as jnp
from jax import lax
from jax.experimental import pallas as pl
from jax.experimental.pallas import tpu as pltpu
from jax.sharding import PartitionSpec as P

SWEEPS = 3

KELVIN_A = 1.0 / (1024.0 * math.pi)
KELVIN_B = KELVIN_A / 3.0
SMOOTH = 0.1
RELAXATION = 0.5

F32 = jnp.float32
BF16 = jnp.bfloat16
MESH = pl.DeviceIdType.MESH
OWN = 128


def hops(step):
    return min(step % 4, 4 - step % 4)


SOURCE_STEPS = sorted(
    ((dz, dy) for dz in range(4) for dy in range(4)),
    key=lambda step: (hops(step[0]) + hops(step[1]), step),
)
TARGET_STEPS = [(2, 0), (2, 1), (1, 0), (1, 1), (3, 0), (3, 1), (0, 1), (0, 0)]
SLOTS = len(SOURCE_STEPS)
BLOCKS = len(TARGET_STEPS)
SOURCES = SLOTS * OWN
COMPONENTS = 6


def lane_gather(values, index):
    numbers = lax.GatherDimensionNumbers(
        offset_dims=(),
        collapsed_slice_dims=(1,),
        start_index_map=(1,),
        operand_batching_dims=(0,),
        start_indices_batching_dims=(0,),
    )
    return lax.gather(
        values,
        index[:, :, None],
        numbers,
        (1, 1),
        mode=lax.GatherScatterMode.PROMISE_IN_BOUNDS,
    )


def brick_side(refs, half, trac_ref, fem_ref):
    nodal, connect, size, shear, bulk, cohesion, friction, active, brick, face = refs
    node_brick = brick[pl.ds(half, 1), :]
    node_face = face[pl.ds(half, 1), :]
    high = jnp.broadcast_to(node_brick // 128, (8, OWN))
    low = jnp.broadcast_to(node_brick % 128, (8, OWN))

    def pick_corner(tile, corners):
        part = connect[:, pl.ds(pl.multiple_of(tile * 128, 128), 128)]
        return jnp.where(high == tile, lane_gather(part, low), corners)

    corners = lax.fori_loop(0, 32, pick_corner, jnp.zeros((8, OWN), jnp.int32), unroll=8)
    row = lax.broadcasted_iota(jnp.int32, (8, OWN), 0)

    def pick(values):
        total = jnp.zeros((8, OWN), F32)
        for group in range(4):
            part = lane_gather(values[8 * group : 8 * group + 8], low)
            total = total + jnp.where(high == row + 8 * group, part, 0.0)
        return jnp.sum(total, axis=0, keepdims=True)

    size_at = pick(size[...])
    shear_at = pick(shear[...])
    bulk_at = pick(bulk[...])
    cohesion_at = pick(cohesion[...])
    friction_at = pick(friction[...])
    active_at = pick(jnp.where(active[...] == 1, 1.0, 0.0))

    corner_high = [jnp.broadcast_to(corners[c : c + 1] // 128, (8, OWN)) for c in range(8)]
    corner_low = [jnp.broadcast_to(corners[c : c + 1] % 128, (8, OWN)) for c in range(8)]

    def pick_nodes(tile, picked):
        columns = pl.ds(pl.multiple_of(tile * 128, 128), 128)
        parts = [nodal[i, :, columns] for i in range(3)]
        out = []
        for c in range(8):
            here = corner_high[c] == tile
            for i in range(3):
                out.append(
                    jnp.where(here, lane_gather(parts[i], corner_low[c]), picked[3 * c + i])
                )
        return tuple(out)

    zero = jnp.zeros((8, OWN), F32)
    picked = lax.fori_loop(0, 32, pick_nodes, (zero,) * 24)

    gradient = [[zero] * 3 for _ in range(3)]
    centre = [zero] * 3
    for c in range(8):
        for i in range(3):
            value = picked[3 * c + i]
            centre[i] = centre[i] + value
            for j in range(3):
                if (c >> j) & 1:
                    gradient[i][j] = gradient[i][j] + value
                else:
                    gradient[i][j] = gradient[i][j] - value
    divisor = 4.0 * size_at
    gradient = [[g / divisor for g in line] for line in gradient]
    centre = [value / 8.0 for value in centre]
    strain = [[0.5 * (gradient[i][j] + gradient[j][i]) for j in range(3)] for i in range(3)]
    volume = strain[0][0] + strain[1][1] + strain[2][2]
    pressure = bulk_at * volume
    third = volume / 3.0
    deviator = [
        [2.0 * shear_at * (strain[i][j] - (third if i == j else 0.0)) for j in range(3)]
        for i in range(3)
    ]
    second = zero
    for i in range(3):
        for j in range(3):
            second = second + deviator[i][j] * deviator[i][j]
    second = 0.5 * second
    scaling = jnp.maximum(cohesion_at - friction_at * pressure, SMOOTH) / jnp.sqrt(
        second + SMOOTH * SMOOTH
    )
    scaling = jnp.where(active_at == 1.0, scaling, 1.0)
    axis_of = node_face // 2
    sign = (1 - 2 * (node_face % 2)).astype(F32)
    for i in range(3):
        line = [scaling * deviator[i][k] + (pressure if i == k else 0.0) for k in range(3)]
        chosen = jnp.where(axis_of == 0, line[0], jnp.where(axis_of == 1, line[1], line[2]))
        trac_ref[i] = (chosen * sign).astype(BF16).astype(F32)
        fem_ref[i] = centre[i].astype(BF16).astype(F32)


def kelvin_components(source, target):
    sx, sy, sz, spread, spread_more = source
    dx, dy, dz = target[0] - sx, target[1] - sy, target[2] - sz
    xx, yy, zz = dx * dx, dy * dy, dz * dz
    squared = ((xx + yy) + zz) + spread
    common = squared + (squared + spread_more)
    inverse = lax.rsqrt(squared)
    weight = (inverse * inverse) * (inverse * KELVIN_B)
    wx, wy = weight * dx, weight * dy
    return (
        weight * (xx + common),
        wx * dy,
        wx * dz,
        weight * (yy + common),
        wy * dz,
        weight * (zz + common),
    )


def kernel(
    nodal_hbm,
    connect_hbm,
    size_ref,
    shear_ref,
    bulk_ref,
    cohesion_ref,
    friction_ref,
    active_ref,
    brick_ref,
    face_ref,
    coords_ref,
    radius_ref,
    stiffness_ref,
    out_ref,
    nodal,
    connect,
    own_place,
    source_place,
    target_place,
    source_wide,
    tile,
    density,
    partial,
    arrived,
    trac,
    fem,
    result,
    local_sem,
    place_send,
    place_recv,
    target_send,
    target_recv,
    density_send,
    density_recv,
    partial_send,
    partial_recv,
    result_send,
    result_recv,
):
    half = lax.axis_index("segment")
    blk = lax.axis_index("blk")
    rows = lax.axis_index("rows")
    z, y = blk // 2, (blk % 2) * 2 + half
    x, core = rows // 2, rows % 2

    def source_peer(slot):
        dz, dy = SOURCE_STEPS[slot]
        pz, py = (z + dz) % 4, (y + dy) % 4
        return (py % 2, pz * 2 + py // 2, rows)

    def target_peer(block, sign=1):
        dx, dc = TARGET_STEPS[block]
        px, pc = (x + 4 + sign * dx) % 4, (core + dc) % 2
        return (half, blk, px * 2 + pc)

    load_nodal = pltpu.make_async_copy(nodal_hbm, nodal, local_sem.at[0])
    load_connect = pltpu.make_async_copy(connect_hbm, connect, local_sem.at[1])
    load_connect.start()
    load_nodal.start()

    barrier = pltpu.get_barrier_semaphore()
    for slot in range(1, SLOTS):
        pl.semaphore_signal(barrier, inc=1, device_id=source_peer(slot), device_id_type=MESH)
    for block in range(BLOCKS - 1):
        pl.semaphore_signal(barrier, inc=1, device_id=target_peer(block), device_id_type=MESH)

    own = pl.ds(pl.multiple_of(half * OWN, OWN), OWN)
    radius = radius_ref[pl.ds(half, 1), :]
    own_place[0:3, :] = coords_ref[:, own]
    own_place[3:4, :] = radius * radius
    own_place[4:8, :] = jnp.zeros((4, OWN), F32)
    source_place[0] = own_place[...]
    target_place[BLOCKS - 1] = own_place[...]

    pl.semaphore_wait(barrier, SLOTS - 1 + BLOCKS - 1)

    def place_copy(slot):
        return pltpu.make_async_remote_copy(
            src_ref=own_place,
            dst_ref=source_place.at[slot],
            send_sem=place_send.at[slot],
            recv_sem=place_recv.at[slot],
            device_id=source_peer(slot),
            device_id_type=MESH,
        )

    def target_copy(block):
        return pltpu.make_async_remote_copy(
            src_ref=own_place,
            dst_ref=target_place.at[block],
            send_sem=target_send.at[block],
            recv_sem=target_recv.at[block],
            device_id=target_peer(block, -1),
            device_id_type=MESH,
        )

    def density_copy(sweep, slot):
        return pltpu.make_async_remote_copy(
            src_ref=density.at[sweep, 0],
            dst_ref=density.at[sweep, slot],
            send_sem=density_send.at[sweep, slot],
            recv_sem=density_recv.at[sweep, slot],
            device_id=source_peer(slot),
            device_id_type=MESH,
        )

    def partial_copy(sweep, block):
        return pltpu.make_async_remote_copy(
            src_ref=partial.at[sweep, block],
            dst_ref=arrived.at[sweep, block],
            send_sem=partial_send.at[sweep, block],
            recv_sem=partial_recv.at[sweep, block],
            device_id=target_peer(block),
            device_id_type=MESH,
        )

    for slot in range(1, SLOTS):
        place_copy(slot).start()
    for block in range(BLOCKS - 1):
        target_copy(block).start()

    def publish(sweep, values):
        density[sweep, 0] = jnp.concatenate(
            [values[0], values[1], values[2], values[0]], axis=0
        ).astype(BF16)
        for slot in range(1, SLOTS):
            density_copy(sweep, slot).start()

    load_connect.wait()
    load_nodal.wait()
    brick_side(
        (
            nodal,
            connect,
            size_ref,
            shear_ref,
            bulk_ref,
            cohesion_ref,
            friction_ref,
            active_ref,
            brick_ref,
            face_ref,
        ),
        half,
        trac,
        fem,
    )
    publish(0, [trac[i] for i in range(3)])

    for slot in range(1, SLOTS):
        place_copy(slot).wait()
    for block in range(BLOCKS - 1):
        target_copy(block).wait()

    @pl.loop(0, SLOTS)
    def _(slot):
        columns = jnp.transpose(source_place[slot])
        place = pl.ds(pl.multiple_of(slot * OWN, OWN), OWN)
        for i in range(4):
            wide = jnp.broadcast_to(columns[:, i : i + 1], (OWN, 128))
            source_wide[i, place, :] = wide
            if i == 3:
                source_wide[4, place, :] = 1.5 * wide

    @pl.loop(0, BLOCKS)
    def _(block):
        target = [
            jnp.broadcast_to(target_place[block, i : i + 1, :], (16, OWN)) for i in range(3)
        ]

        @pl.loop(0, SOURCES // 128)
        def _(chunk):
            for step in range(8):
                place = pl.ds(pl.multiple_of(chunk * 128 + step * 16, 16), 16)
                source = [source_wide[i, place, :] for i in range(5)]
                values = kelvin_components(source, target)
                for k in range(COMPONENTS):
                    tile[k, block, place, :] = values[k].astype(BF16)

    @pl.loop(0, SWEEPS)
    def _(sweep):
        for slot in range(1, SLOTS):
            density_copy(sweep, slot).wait_recv()
        xy = jnp.concatenate([density[sweep, slot, 0:16, :] for slot in range(SLOTS)], axis=1)
        zx = jnp.concatenate([density[sweep, slot, 16:32, :] for slot in range(SLOTS)], axis=1)
        xyz = jnp.concatenate([xy, zx], axis=0)
        for pair in range(0, BLOCKS, 2):

            def product(left, k):
                right = jnp.concatenate([tile[k, pair], tile[k, pair + 1]], axis=1)
                return jnp.dot(left, right, preferred_element_type=F32)

            p_xx = product(xy, 0)
            p_xy = product(xy, 1)
            p_xz = product(zx, 2)
            p_yy = product(xy, 3)
            p_yz = product(xyz, 4)
            p_zz = product(zx, 5)
            g_x = p_xx[0:8] + p_xy[8:16] + p_xz[0:8]
            g_y = p_xy[0:8] + p_yy[8:16] + p_yz[16:24]
            g_z = p_xz[8:16] + p_yz[8:16] + p_zz[0:8]
            for block in (pair, pair + 1):
                lanes = slice((block - pair) * OWN, (block - pair + 1) * OWN)
                partial[sweep, block, 0] = g_x[:, lanes]
                partial[sweep, block, 1] = g_y[:, lanes]
                partial[sweep, block, 2] = g_z[:, lanes]
                if block < BLOCKS - 1:
                    partial_copy(sweep, block).start()
        total = [partial[sweep, BLOCKS - 1, i] for i in range(3)]
        for block in range(BLOCKS - 1):
            partial_copy(sweep, block).wait_recv()
            for i in range(3):
                total[i] = total[i] + arrived[sweep, block, i]

        @pl.when(sweep < SWEEPS - 1)
        def _():
            stiffness = stiffness_ref[pl.ds(half, 1), :]
            publish(sweep + 1, [trac[i] - stiffness * total[i] for i in range(3)])

        @pl.when(sweep == SWEEPS - 1)
        def _():
            for i in range(3):
                fem_wide = fem[i]
                result[half, i] = fem_wide + RELAXATION * (total[i] - fem_wide)

    exchange = pltpu.make_async_remote_copy(
        src_ref=result.at[half],
        dst_ref=result.at[half],
        send_sem=result_send,
        recv_sem=result_recv,
        device_id=((half + 1) % 2, blk, rows),
        device_id_type=MESH,
    )
    exchange.start()

    @pl.loop(0, SWEEPS)
    def _(sweep):
        for slot in range(1, SLOTS):
            density_copy(sweep, slot).wait_send()
        for block in range(BLOCKS - 1):
            partial_copy(sweep, block).wait_send()

    exchange.wait()
    for i in range(3):
        out_ref[i] = jnp.concatenate([result[0, i], result[1, i]], axis=1)


def on_device(
    nodal_disp,
    connect,
    brick_size,
    shear_modulus,
    bulk_modulus,
    cohesion,
    friction,
    active,
    patch_brick,
    patch_face,
    coords,
    radius,
    stiffness,
):
    batches = nodal_disp.shape[0]
    local_nodes = coords.shape[1]
    anywhere = pl.BlockSpec(memory_space=pl.ANY)
    vmem = pl.BlockSpec(memory_space=pltpu.VMEM)
    dma = pltpu.SemaphoreType.DMA
    by_brick = [
        values.reshape(-1, 128)
        for values in (brick_size, shear_modulus, bulk_modulus, cohesion, friction, active)
    ]
    by_node = [values.reshape(-1, OWN) for values in (patch_brick, patch_face)]
    relaxed = pl.pallas_call(
        kernel,
        out_shape=jax.ShapeDtypeStruct((3, batches, local_nodes), F32),
        in_specs=[anywhere] * 2 + [vmem] * 11,
        out_specs=vmem,
        scratch_shapes=[
            pltpu.VMEM((3, batches, nodal_disp.shape[2]), F32),
            pltpu.VMEM(connect.shape, jnp.int32),
            pltpu.VMEM((8, OWN), F32),
            pltpu.VMEM((SLOTS, 8, OWN), F32),
            pltpu.VMEM((BLOCKS, 8, OWN), F32),
            pltpu.VMEM((5, SOURCES, 128), F32),
            pltpu.VMEM((COMPONENTS, BLOCKS, SOURCES, 128), BF16),
            pltpu.VMEM((SWEEPS, SLOTS, 32, OWN), BF16),
            pltpu.VMEM((SWEEPS, BLOCKS, 3, 8, OWN), F32),
            pltpu.VMEM((SWEEPS, BLOCKS, 3, 8, OWN), F32),
            pltpu.VMEM((3, 8, OWN), F32),
            pltpu.VMEM((3, 8, OWN), F32),
            pltpu.VMEM((2, 3, 8, OWN), F32),
            dma((2,)),
            dma((SLOTS,)),
            dma((SLOTS,)),
            dma((BLOCKS,)),
            dma((BLOCKS,)),
            dma((SWEEPS, SLOTS)),
            dma((SWEEPS, SLOTS)),
            dma((SWEEPS, BLOCKS)),
            dma((SWEEPS, BLOCKS)),
            dma,
            dma,
        ],
        compiler_params=pltpu.CompilerParams(
            collective_id=0, has_side_effects=True, vmem_limit_bytes=50 * 2**20
        ),
    )(
        nodal_disp.transpose(1, 0, 2),
        connect,
        *by_brick,
        *by_node,
        coords,
        radius.reshape(-1, OWN),
        stiffness.reshape(-1, OWN),
    )
    return relaxed.transpose(1, 0, 2)


def solution(mesh):
    split = ("blk", "rows")
    return jax.shard_map(
        on_device,
        mesh=mesh,
        in_specs=(
            P(None, None, split),
            P(None, split),
            P(split),
            P(split),
            P(split),
            P(split),
            P(split),
            P(split),
            P(split),
            P(split),
            P(None, split),
            P(split),
            P(split),
        ),
        out_specs=P(None, None, split),
        check_vma=False,
    )
```

```python
import math

import jax
import jax.numpy as jnp
from jax import lax
from jax.experimental import pallas as pl
from jax.experimental.pallas import tpu as pltpu
from jax.sharding import PartitionSpec as P

SWEEPS = 3

KELVIN_A = 1.0 / (1024.0 * math.pi)
KELVIN_B = KELVIN_A / 3.0
SMOOTH = 0.1
RELAXATION = 0.5

F32 = jnp.float32
BF16 = jnp.bfloat16
MESH = pl.DeviceIdType.MESH
OWN = 128


def hops(step):
    return min(step % 4, 4 - step % 4)


SOURCE_STEPS = sorted(
    ((dz, dy) for dz in range(4) for dy in range(4)),
    key=lambda step: (hops(step[0]) + hops(step[1]), step),
)
TARGET_STEPS = [(2, 0), (2, 1), (1, 0), (1, 1), (3, 0), (3, 1), (0, 1), (0, 0)]
SLOTS = len(SOURCE_STEPS)
BLOCKS = len(TARGET_STEPS)
SOURCES = SLOTS * OWN
PAIRS = BLOCKS // 2
CHUNKS = SLOTS // 2
NEAR = 2
GROUPS = ((0, 2), (2, 6))
COMPONENTS = 6


def lane_gather(values, index):
    numbers = lax.GatherDimensionNumbers(
        offset_dims=(),
        collapsed_slice_dims=(1,),
        start_index_map=(1,),
        operand_batching_dims=(0,),
        start_indices_batching_dims=(0,),
    )
    return lax.gather(
        values,
        index[:, :, None],
        numbers,
        (1, 1),
        mode=lax.GatherScatterMode.PROMISE_IN_BOUNDS,
    )


def brick_side(refs, half, trac_ref, fem_ref):
    nodal, connect, size, shear, bulk, cohesion, friction, active, brick, face = refs
    node_brick = brick[pl.ds(half, 1), :]
    node_face = face[pl.ds(half, 1), :]
    high = jnp.broadcast_to(node_brick // 128, (8, OWN))
    low = jnp.broadcast_to(node_brick % 128, (8, OWN))

    def pick_corner(tile, corners):
        part = connect[:, pl.ds(pl.multiple_of(tile * 128, 128), 128)]
        return jnp.where(high == tile, lane_gather(part, low), corners)

    corners = lax.fori_loop(0, 32, pick_corner, jnp.zeros((8, OWN), jnp.int32), unroll=16)
    row = lax.broadcasted_iota(jnp.int32, (8, OWN), 0)

    def pick(values):
        total = jnp.zeros((8, OWN), F32)
        for group in range(4):
            part = lane_gather(values[8 * group : 8 * group + 8], low)
            total = total + jnp.where(high == row + 8 * group, part, 0.0)
        return jnp.sum(total, axis=0, keepdims=True)

    size_at = pick(size[...])
    shear_at = pick(shear[...])
    bulk_at = pick(bulk[...])
    cohesion_at = pick(cohesion[...])
    friction_at = pick(friction[...])
    active_at = pick(jnp.where(active[...] == 1, 1.0, 0.0))

    corner_high = [jnp.broadcast_to(corners[c : c + 1] // 128, (8, OWN)) for c in range(8)]
    corner_low = [jnp.broadcast_to(corners[c : c + 1] % 128, (8, OWN)) for c in range(8)]

    zero = jnp.zeros((8, OWN), F32)
    picked = []
    for c in range(8):

        def pick_nodes(tile, values, c=c):
            columns = pl.ds(pl.multiple_of(tile * 128, 128), 128)
            here = corner_high[c] == tile
            return tuple(
                jnp.where(here, lane_gather(nodal[i, :, columns], corner_low[c]), values[i])
                for i in range(3)
            )

        picked.extend(lax.fori_loop(0, 32, pick_nodes, (zero,) * 3, unroll=16))

    gradient = [[zero] * 3 for _ in range(3)]
    centre = [zero] * 3
    for c in range(8):
        for i in range(3):
            value = picked[3 * c + i]
            centre[i] = centre[i] + value
            for j in range(3):
                if (c >> j) & 1:
                    gradient[i][j] = gradient[i][j] + value
                else:
                    gradient[i][j] = gradient[i][j] - value
    divisor = 4.0 * size_at
    gradient = [[g / divisor for g in line] for line in gradient]
    centre = [value / 8.0 for value in centre]
    strain = [[0.5 * (gradient[i][j] + gradient[j][i]) for j in range(3)] for i in range(3)]
    volume = strain[0][0] + strain[1][1] + strain[2][2]
    pressure = bulk_at * volume
    third = volume / 3.0
    deviator = [
        [2.0 * shear_at * (strain[i][j] - (third if i == j else 0.0)) for j in range(3)]
        for i in range(3)
    ]
    second = zero
    for i in range(3):
        for j in range(3):
            second = second + deviator[i][j] * deviator[i][j]
    second = 0.5 * second
    scaling = jnp.maximum(cohesion_at - friction_at * pressure, SMOOTH) / jnp.sqrt(
        second + SMOOTH * SMOOTH
    )
    scaling = jnp.where(active_at == 1.0, scaling, 1.0)
    axis_of = node_face // 2
    sign = (1 - 2 * (node_face % 2)).astype(F32)
    for i in range(3):
        line = [scaling * deviator[i][k] + (pressure if i == k else 0.0) for k in range(3)]
        chosen = jnp.where(axis_of == 0, line[0], jnp.where(axis_of == 1, line[1], line[2]))
        trac_ref[i] = (chosen * sign).astype(BF16).astype(F32)
        fem_ref[0, i] = centre[i].astype(BF16).astype(F32)


def kelvin_components(source, target):
    sx, sy, sz, spread, spread_more = source
    dx, dy, dz = target[0] - sx, target[1] - sy, target[2] - sz
    xx, yy, zz = dx * dx, dy * dy, dz * dz
    squared = ((xx + yy) + zz) + spread
    common = squared + (squared + spread_more)
    inverse = lax.rsqrt(squared)
    weight = (inverse * inverse) * (inverse * KELVIN_B)
    wx, wy = weight * dx, weight * dy
    return (
        weight * (xx + common),
        wx * dy,
        wx * dz,
        weight * (yy + common),
        wy * dz,
        weight * (zz + common),
    )


def kernel(
    nodal_hbm,
    connect_hbm,
    size_hbm,
    shear_hbm,
    bulk_hbm,
    cohesion_hbm,
    friction_hbm,
    active_hbm,
    brick_hbm,
    face_hbm,
    coords_hbm,
    radius_hbm,
    stiffness_hbm,
    out_ref,
    nodal,
    connect,
    size_ref,
    shear_ref,
    bulk_ref,
    cohesion_ref,
    friction_ref,
    active_ref,
    brick_ref,
    face_ref,
    coords_ref,
    radius_ref,
    stiffness_ref,
    own_place,
    source_place,
    target_place,
    source_wide,
    tile,
    density,
    partial,
    arrived,
    trac,
    fem,
    beside,
    local_sem,
    place_send,
    place_recv,
    target_send,
    target_recv,
    density_send,
    density_recv,
    partial_send,
    partial_recv,
    beside_send,
    beside_recv,
    fem_send,
    fem_recv,
):
    half = lax.axis_index("segment")
    blk = lax.axis_index("blk")
    rows = lax.axis_index("rows")
    z, y = blk // 2, (blk % 2) * 2 + half
    x, core = rows // 2, rows % 2

    def source_peer(slot):
        dz, dy = SOURCE_STEPS[slot]
        pz, py = (z + dz) % 4, (y + dy) % 4
        return (py % 2, pz * 2 + py // 2, rows)

    def target_peer(block, sign=1):
        dx, dc = TARGET_STEPS[block]
        px, pc = (x + 4 + sign * dx) % 4, (core + dc) % 2
        return (half, blk, px * 2 + pc)

    def beside_peer(block):
        _, _, peer_rows = target_peer(block)
        return ((half + 1) % 2, blk, peer_rows)

    place_loads = [(coords_hbm, coords_ref), (radius_hbm, radius_ref)]
    brick_loads = [
        (brick_hbm, brick_ref),
        (connect_hbm, connect),
        (nodal_hbm, nodal),
        (face_hbm, face_ref),
        (size_hbm, size_ref),
        (shear_hbm, shear_ref),
        (bulk_hbm, bulk_ref),
        (cohesion_hbm, cohesion_ref),
        (friction_hbm, friction_ref),
        (active_hbm, active_ref),
        (stiffness_hbm, stiffness_ref),
    ]
    loads = [
        pltpu.make_async_copy(source, target, local_sem.at[i])
        for i, (source, target) in enumerate(place_loads + brick_loads)
    ]
    for load in loads:
        load.start()

    barrier = pltpu.get_barrier_semaphore()
    for slot in range(1, SLOTS):
        pl.semaphore_signal(barrier, inc=1, device_id=source_peer(slot), device_id_type=MESH)
    for block in range(BLOCKS - 1):
        pl.semaphore_signal(barrier, inc=1, device_id=target_peer(block), device_id_type=MESH)
        pl.semaphore_signal(barrier, inc=1, device_id=beside_peer(block), device_id_type=MESH)

    for load in loads[: len(place_loads)]:
        load.wait()
    own = pl.ds(pl.multiple_of(half * OWN, OWN), OWN)
    radius = radius_ref[pl.ds(half, 1), :]
    own_place[0:3, :] = coords_ref[:, own]
    own_place[3:4, :] = radius * radius
    own_place[4:8, :] = jnp.zeros((4, OWN), F32)
    source_place[0] = own_place[...]
    target_place[BLOCKS - 1] = own_place[...]

    for load in loads[len(place_loads) :]:
        load.wait()

    def place_copy(slot):
        return pltpu.make_async_remote_copy(
            src_ref=own_place,
            dst_ref=source_place.at[slot],
            send_sem=place_send.at[slot],
            recv_sem=place_recv.at[slot],
            device_id=source_peer(slot),
            device_id_type=MESH,
        )

    def target_copy(block):
        return pltpu.make_async_remote_copy(
            src_ref=own_place,
            dst_ref=target_place.at[block],
            send_sem=target_send.at[block],
            recv_sem=target_recv.at[block],
            device_id=target_peer(block, -1),
            device_id_type=MESH,
        )

    def density_copy(sweep, slot):
        return pltpu.make_async_remote_copy(
            src_ref=density.at[sweep, 0],
            dst_ref=density.at[sweep, slot],
            send_sem=density_send.at[sweep, slot],
            recv_sem=density_recv.at[sweep, slot],
            device_id=source_peer(slot),
            device_id_type=MESH,
        )

    def partial_copy(sweep, block):
        return pltpu.make_async_remote_copy(
            src_ref=partial.at[sweep, block],
            dst_ref=arrived.at[sweep, block],
            send_sem=partial_send.at[sweep, block],
            recv_sem=partial_recv.at[sweep, block],
            device_id=target_peer(block),
            device_id_type=MESH,
        )

    def beside_copy(block):
        return pltpu.make_async_remote_copy(
            src_ref=partial.at[SWEEPS - 1, block],
            dst_ref=beside.at[block],
            send_sem=beside_send.at[block],
            recv_sem=beside_recv.at[block],
            device_id=beside_peer(block),
            device_id_type=MESH,
        )

    def fem_copy():
        return pltpu.make_async_remote_copy(
            src_ref=fem.at[0],
            dst_ref=fem.at[1],
            send_sem=fem_send,
            recv_sem=fem_recv,
            device_id=beside_peer(BLOCKS - 1),
            device_id_type=MESH,
        )

    def send_density(sweep, values):
        density[sweep, 0] = jnp.concatenate(
            [values[0], values[1], values[2], values[0]], axis=0
        ).astype(BF16)

        def start():
            for slot in reversed(range(1, SLOTS)):
                density_copy(sweep, slot).start()

        return start

    def widen(slot):
        columns = jnp.transpose(source_place[slot])
        place = pl.ds(pl.multiple_of(slot * OWN, OWN), OWN)
        for i in range(4):
            wide = jnp.broadcast_to(columns[:, i : i + 1], (OWN, 128))
            source_wide[i, place, :] = wide
            if i == 3:
                source_wide[4, place, :] = 1.5 * wide

    def tile_piece(pair, chunk):
        for block in (2 * pair, 2 * pair + 1):
            target = [
                jnp.broadcast_to(target_place[block, i : i + 1, :], (16, OWN)) for i in range(3)
            ]

            @pl.loop(0, 2)
            def _(part):
                for step in range(8):
                    first = chunk * 256 + part * 128 + step * 16
                    place = pl.ds(pl.multiple_of(first, 16), 16)
                    source = [source_wide[i, place, :] for i in range(5)]
                    values = kelvin_components(source, target)
                    for k in range(COMPONENTS):
                        tile[k, block, place, :] = values[k].astype(BF16)

    def product(sweep, blocks, chunk, chunks):
        slots = range(2 * chunks)
        xy = jnp.concatenate([density[sweep, 2 * chunk + i, 0:16, :] for i in slots], axis=1)
        zx = jnp.concatenate([density[sweep, 2 * chunk + i, 16:32, :] for i in slots], axis=1)
        xyz = jnp.concatenate([xy, zx], axis=0)
        place = pl.ds(pl.multiple_of(chunk * 256, 256), chunks * 256)

        def dot(left, k):
            right = jnp.concatenate([tile[k, block, place, :] for block in blocks], axis=1)
            return jnp.dot(left, right, preferred_element_type=F32)

        p_xx = dot(xy, 0)
        p_xy = dot(xy, 1)
        p_xz = dot(zx, 2)
        p_yy = dot(xy, 3)
        p_yz = dot(xyz, 4)
        p_zz = dot(zx, 5)
        return (
            p_xx[0:8] + p_xy[8:16] + p_xz[0:8],
            p_xy[0:8] + p_yy[8:16] + p_yz[16:24],
            p_xz[8:16] + p_yz[8:16] + p_zz[0:8],
        )

    def accumulate(sweep, blocks, sums, first):
        for part, block in enumerate(blocks):
            for i in range(3):
                value = sums[i][:, part * OWN : (part + 1) * OWN]
                if not first:
                    value = value + partial[sweep, block, i]
                partial[sweep, block, i] = value

    def send_partial(sweep, blocks):
        for block in blocks:
            if block < BLOCKS - 1:
                partial_copy(sweep, block).start()

    def total_of(sweep):
        total = [partial[sweep, BLOCKS - 1, i] for i in range(3)]
        for block in reversed(range(BLOCKS - 1)):
            partial_copy(sweep, block).wait_recv()
            for i in range(3):
                total[i] = total[i] + arrived[sweep, block, i]
        return total

    stiffness = stiffness_ref[pl.ds(half, 1), :]

    def next_density(sweep):
        total = total_of(sweep)
        send_density(sweep + 1, [trac[i] - stiffness * total[i] for i in range(3)])()

    brick_side(
        (
            nodal,
            connect,
            size_ref,
            shear_ref,
            bulk_ref,
            cohesion_ref,
            friction_ref,
            active_ref,
            brick_ref,
            face_ref,
        ),
        half,
        trac,
        fem,
    )
    start_density = send_density(0, [trac[i] for i in range(3)])
    widen(0)

    pl.semaphore_wait(barrier, SLOTS - 1 + 2 * (BLOCKS - 1))

    for slot in range(1, 2 * NEAR):
        place_copy(slot).start()
    for block in range(BLOCKS - 1):
        target_copy(block).start()
    for slot in reversed(range(2 * NEAR, SLOTS)):
        place_copy(slot).start()
    start_density()
    fem_copy().start()

    for slot in range(1, 2 * NEAR):
        place_copy(slot).wait_recv()

    for slot in range(1, 2 * NEAR):
        widen(slot)

    for block in range(BLOCKS - 1):
        target_copy(block).wait_recv()

    @pl.loop(0, PAIRS)
    def _(pair):
        @pl.loop(0, NEAR)
        def _(chunk):
            tile_piece(pair, chunk)

    for slot in range(2 * NEAR, SLOTS):
        place_copy(slot).wait_recv()

    @pl.loop(2 * NEAR, SLOTS, step=4)
    def _(slot):
        for i in range(4):
            widen(slot + i)

    for slot in range(1, SLOTS):
        density_copy(0, slot).wait_recv()

    for pair in range(PAIRS):

        @pl.loop(NEAR, CHUNKS)
        def _(chunk):
            tile_piece(pair, chunk)

        blocks = (2 * pair, 2 * pair + 1)
        accumulate(0, blocks, product(0, blocks, 0, CHUNKS), True)
        send_partial(0, blocks)

    next_density(0)

    @pl.loop(1, SWEEPS)
    def _(sweep):
        for first, chunks in GROUPS:
            for slot in range(max(1, 2 * first), 2 * (first + chunks)):
                density_copy(sweep, slot).wait_recv()
            if first + chunks < CHUNKS:
                every = range(BLOCKS)
                accumulate(sweep, every, product(sweep, every, first, chunks), first == 0)
            else:
                for pair in range(PAIRS):
                    blocks = (2 * pair, 2 * pair + 1)
                    accumulate(sweep, blocks, product(sweep, blocks, first, chunks), False)

                    @pl.when(sweep == SWEEPS - 1)
                    def _():
                        for block in blocks:
                            beside_copy(block).start()

                    send_partial(sweep, blocks)

        @pl.when(sweep < SWEEPS - 1)
        def _():
            next_density(sweep)

    for slot in range(1, SLOTS):
        place_copy(slot).wait_send()
    for block in range(BLOCKS - 1):
        target_copy(block).wait_send()
    fem_copy().wait()

    @pl.loop(0, SWEEPS)
    def _(sweep):
        for slot in range(1, SLOTS):
            density_copy(sweep, slot).wait_send()
        for block in range(BLOCKS - 1):
            partial_copy(sweep, block).wait_send()

    own_total = total_of(SWEEPS - 1)
    for block in range(BLOCKS):
        beside_copy(block).wait_send()
    other_total = [jnp.zeros((8, OWN), F32)] * 3
    for block in reversed(range(BLOCKS)):
        beside_copy(block).wait_recv()
        for i in range(3):
            other_total[i] = other_total[i] + beside[block, i]
    for i in range(3):
        own_out = fem[0, i] + RELAXATION * (own_total[i] - fem[0, i])
        other_out = fem[1, i] + RELAXATION * (other_total[i] - fem[1, i])
        low = jnp.where(half == 0, own_out, other_out)
        high = jnp.where(half == 0, other_out, own_out)
        out_ref[i] = jnp.concatenate([low, high], axis=1)


def on_device(
    nodal_disp,
    connect,
    brick_size,
    shear_modulus,
    bulk_modulus,
    cohesion,
    friction,
    active,
    patch_brick,
    patch_face,
    coords,
    radius,
    stiffness,
):
    batches = nodal_disp.shape[0]
    local_nodes = coords.shape[1]
    anywhere = pl.BlockSpec(memory_space=pl.ANY)
    vmem = pl.BlockSpec(memory_space=pltpu.VMEM)
    dma = pltpu.SemaphoreType.DMA
    by_brick = [
        values.reshape(-1, 128)
        for values in (brick_size, shear_modulus, bulk_modulus, cohesion, friction, active)
    ]
    by_node = [values.reshape(-1, OWN) for values in (patch_brick, patch_face)]
    inputs = (
        nodal_disp.transpose(1, 0, 2),
        connect,
        *by_brick,
        *by_node,
        coords,
        radius.reshape(-1, OWN),
        stiffness.reshape(-1, OWN),
    )
    relaxed = pl.pallas_call(
        kernel,
        out_shape=jax.ShapeDtypeStruct((3, batches, local_nodes), F32),
        in_specs=[anywhere] * len(inputs),
        out_specs=vmem,
        scratch_shapes=[
            *(pltpu.VMEM(values.shape, values.dtype) for values in inputs),
            pltpu.VMEM((8, OWN), F32),
            pltpu.VMEM((SLOTS, 8, OWN), F32),
            pltpu.VMEM((BLOCKS, 8, OWN), F32),
            pltpu.VMEM((5, SOURCES, 128), F32),
            pltpu.VMEM((COMPONENTS, BLOCKS, SOURCES, 128), BF16),
            pltpu.VMEM((SWEEPS, SLOTS, 32, OWN), BF16),
            pltpu.VMEM((SWEEPS, BLOCKS, 3, 8, OWN), F32),
            pltpu.VMEM((SWEEPS, BLOCKS, 3, 8, OWN), F32),
            pltpu.VMEM((3, 8, OWN), F32),
            pltpu.VMEM((2, 3, 8, OWN), F32),
            pltpu.VMEM((BLOCKS, 3, 8, OWN), F32),
            dma((len(inputs),)),
            dma((SLOTS,)),
            dma((SLOTS,)),
            dma((BLOCKS,)),
            dma((BLOCKS,)),
            dma((SWEEPS, SLOTS)),
            dma((SWEEPS, SLOTS)),
            dma((SWEEPS, BLOCKS)),
            dma((SWEEPS, BLOCKS)),
            dma((BLOCKS,)),
            dma((BLOCKS,)),
            dma,
            dma,
        ],
        compiler_params=pltpu.CompilerParams(
            collective_id=0, has_side_effects=True, vmem_limit_bytes=60 * 2**20
        ),
    )(
        *inputs
    )
    return relaxed.transpose(1, 0, 2)


def solution(mesh):
    split = ("blk", "rows")
    return jax.shard_map(
        on_device,
        mesh=mesh,
        in_specs=(
            P(None, None, split),
            P(None, split),
            P(split),
            P(split),
            P(split),
            P(split),
            P(split),
            P(split),
            P(split),
            P(split),
            P(None, split),
            P(split),
            P(split),
        ),
        out_specs=P(None, None, split),
        check_vma=False,
    )
```

```python
import math

import jax
import jax.numpy as jnp
from jax import lax
from jax.experimental import pallas as pl
from jax.experimental.pallas import tpu as pltpu
from jax.sharding import PartitionSpec as P

SWEEPS = 3

KELVIN_A = 1.0 / (1024.0 * math.pi)
KELVIN_B = KELVIN_A / 3.0
SMOOTH = 0.1
RELAXATION = 0.5

F32 = jnp.float32
BF16 = jnp.bfloat16
MESH = pl.DeviceIdType.MESH
OWN = 128


def hops(step):
    return min(step % 4, 4 - step % 4)


SOURCE_STEPS = sorted(
    ((dz, dy) for dz in range(4) for dy in range(4)),
    key=lambda step: (hops(step[0]) + hops(step[1]), step),
)
TARGET_STEPS = [(2, 0), (2, 1), (1, 0), (1, 1), (3, 0), (3, 1), (0, 1), (0, 0)]
SLOTS = len(SOURCE_STEPS)
BLOCKS = len(TARGET_STEPS)
SOURCES = SLOTS * OWN
PAIRS = BLOCKS // 2
CHUNKS = SLOTS // 2
NEAR = 2
GROUPS = ((0, 2), (2, 6))
COMPONENTS = 6


def lane_gather(values, index):
    numbers = lax.GatherDimensionNumbers(
        offset_dims=(),
        collapsed_slice_dims=(1,),
        start_index_map=(1,),
        operand_batching_dims=(0,),
        start_indices_batching_dims=(0,),
    )
    return lax.gather(
        values,
        index[:, :, None],
        numbers,
        (1, 1),
        mode=lax.GatherScatterMode.PROMISE_IN_BOUNDS,
    )


def brick_side(refs, half, trac_ref, fem_ref):
    nodal, connect, size, shear, bulk, cohesion, friction, active, brick, face = refs
    node_brick = brick[pl.ds(half, 1), :]
    node_face = face[pl.ds(half, 1), :]
    high = jnp.broadcast_to(node_brick // 128, (8, OWN))
    low = jnp.broadcast_to(node_brick % 128, (8, OWN))

    def pick_corner(tile, corners):
        part = connect[:, pl.ds(pl.multiple_of(tile * 128, 128), 128)]
        return jnp.where(high == tile, lane_gather(part, low), corners)

    corners = lax.fori_loop(0, 32, pick_corner, jnp.zeros((8, OWN), jnp.int32), unroll=16)
    row = lax.broadcasted_iota(jnp.int32, (8, OWN), 0)

    def pick(values):
        total = jnp.zeros((8, OWN), F32)
        for group in range(4):
            part = lane_gather(values[8 * group : 8 * group + 8], low)
            total = total + jnp.where(high == row + 8 * group, part, 0.0)
        return jnp.sum(total, axis=0, keepdims=True)

    size_at = pick(size[...])
    shear_at = pick(shear[...])
    bulk_at = pick(bulk[...])
    cohesion_at = pick(cohesion[...])
    friction_at = pick(friction[...])
    active_at = pick(jnp.where(active[...] == 1, 1.0, 0.0))

    corner_high = [jnp.broadcast_to(corners[c : c + 1] // 128, (8, OWN)) for c in range(8)]
    corner_low = [jnp.broadcast_to(corners[c : c + 1] % 128, (8, OWN)) for c in range(8)]

    zero = jnp.zeros((8, OWN), F32)
    picked = []
    for c in range(8):

        def pick_nodes(tile, values, c=c):
            columns = pl.ds(pl.multiple_of(tile * 128, 128), 128)
            here = corner_high[c] == tile
            return tuple(
                jnp.where(here, lane_gather(nodal[i, :, columns], corner_low[c]), values[i])
                for i in range(3)
            )

        picked.extend(lax.fori_loop(0, 32, pick_nodes, (zero,) * 3, unroll=16))

    gradient = [[zero] * 3 for _ in range(3)]
    centre = [zero] * 3
    for c in range(8):
        for i in range(3):
            value = picked[3 * c + i]
            centre[i] = centre[i] + value
            for j in range(3):
                if (c >> j) & 1:
                    gradient[i][j] = gradient[i][j] + value
                else:
                    gradient[i][j] = gradient[i][j] - value
    divisor = 4.0 * size_at
    gradient = [[g / divisor for g in line] for line in gradient]
    centre = [value / 8.0 for value in centre]
    strain = [[0.5 * (gradient[i][j] + gradient[j][i]) for j in range(3)] for i in range(3)]
    volume = strain[0][0] + strain[1][1] + strain[2][2]
    pressure = bulk_at * volume
    third = volume / 3.0
    deviator = [
        [2.0 * shear_at * (strain[i][j] - (third if i == j else 0.0)) for j in range(3)]
        for i in range(3)
    ]
    second = zero
    for i in range(3):
        for j in range(3):
            second = second + deviator[i][j] * deviator[i][j]
    second = 0.5 * second
    scaling = jnp.maximum(cohesion_at - friction_at * pressure, SMOOTH) / jnp.sqrt(
        second + SMOOTH * SMOOTH
    )
    scaling = jnp.where(active_at == 1.0, scaling, 1.0)
    axis_of = node_face // 2
    sign = (1 - 2 * (node_face % 2)).astype(F32)
    for i in range(3):
        line = [scaling * deviator[i][k] + (pressure if i == k else 0.0) for k in range(3)]
        chosen = jnp.where(axis_of == 0, line[0], jnp.where(axis_of == 1, line[1], line[2]))
        trac_ref[i] = (chosen * sign).astype(BF16).astype(F32)
        fem_ref[0, i] = centre[i].astype(BF16).astype(F32)


def kelvin_components(source, target):
    sx, sy, sz, spread, spread_more = source
    dx, dy, dz = target[0] - sx, target[1] - sy, target[2] - sz
    xx, yy, zz = dx * dx, dy * dy, dz * dz
    squared = ((xx + yy) + zz) + spread
    common = squared + (squared + spread_more)
    inverse = lax.rsqrt(squared)
    weight = (inverse * inverse) * (inverse * KELVIN_B)
    wx, wy = weight * dx, weight * dy
    return (
        weight * (xx + common),
        wx * dy,
        wx * dz,
        weight * (yy + common),
        wy * dz,
        weight * (zz + common),
    )


def kernel(
    nodal_hbm,
    connect_hbm,
    size_hbm,
    shear_hbm,
    bulk_hbm,
    cohesion_hbm,
    friction_hbm,
    active_hbm,
    brick_hbm,
    face_hbm,
    coords_hbm,
    radius_hbm,
    stiffness_hbm,
    out_ref,
    nodal,
    connect,
    size_ref,
    shear_ref,
    bulk_ref,
    cohesion_ref,
    friction_ref,
    active_ref,
    brick_ref,
    face_ref,
    coords_ref,
    radius_ref,
    stiffness_ref,
    own_place,
    source_place,
    target_place,
    source_wide,
    tile,
    density,
    partial,
    arrived,
    trac,
    fem,
    beside,
    repeat,
    local_sem,
    place_send,
    place_recv,
    target_send,
    target_recv,
    density_send,
    density_recv,
    partial_send,
    partial_recv,
    beside_send,
    beside_recv,
    fem_send,
    fem_recv,
):
    half = lax.axis_index("segment")
    blk = lax.axis_index("blk")
    rows = lax.axis_index("rows")
    z, y = blk // 2, (blk % 2) * 2 + half
    x, core = rows // 2, rows % 2

    def source_peer(slot):
        dz, dy = SOURCE_STEPS[slot]
        pz, py = (z + dz) % 4, (y + dy) % 4
        return (py % 2, pz * 2 + py // 2, rows)

    def target_peer(block, sign=1):
        dx, dc = TARGET_STEPS[block]
        px, pc = (x + 4 + sign * dx) % 4, (core + dc) % 2
        return (half, blk, px * 2 + pc)

    def beside_peer(block):
        _, _, peer_rows = target_peer(block)
        return ((half + 1) % 2, blk, peer_rows)

    barrier = pltpu.get_barrier_semaphore()
    peers = [source_peer(slot) for slot in reversed(range(1, SLOTS))]
    peers[5:5] = [beside_peer(block) for block in range(BLOCKS - 1)]
    peers += [target_peer(block) for block in range(BLOCKS - 1)]
    for peer in peers:
        pl.semaphore_signal(barrier, inc=1, device_id=peer, device_id_type=MESH)

    place_loads = [(coords_hbm, coords_ref), (radius_hbm, radius_ref)]
    brick_loads = [
        (brick_hbm, brick_ref),
        (connect_hbm, connect),
        (nodal_hbm, nodal),
        (face_hbm, face_ref),
        (size_hbm, size_ref),
        (shear_hbm, shear_ref),
        (bulk_hbm, bulk_ref),
        (cohesion_hbm, cohesion_ref),
        (friction_hbm, friction_ref),
        (active_hbm, active_ref),
        (stiffness_hbm, stiffness_ref),
    ]
    loads = [
        pltpu.make_async_copy(source, target, local_sem.at[i])
        for i, (source, target) in enumerate(place_loads + brick_loads)
    ]
    for load in loads:
        load.start()

    for load in loads[: len(place_loads)]:
        load.wait()
    own = pl.ds(pl.multiple_of(half * OWN, OWN), OWN)
    radius = radius_ref[pl.ds(half, 1), :]
    own_place[0:3, :] = coords_ref[:, own]
    own_place[3:4, :] = radius * radius
    own_place[4:5, :] = 1.5 * (radius * radius)
    own_place[5:8, :] = jnp.zeros((3, OWN), F32)
    row = lax.broadcasted_iota(jnp.int32, repeat.shape, 0)
    column = lax.broadcasted_iota(jnp.int32, repeat.shape, 1)
    repeat[...] = jnp.where((row % 8 == column // 128) & (row < 24), 1.0, 0.0).astype(BF16)
    source_place[0] = own_place[...]
    target_place[BLOCKS - 1] = own_place[...]

    for load in loads[len(place_loads) :]:
        load.wait()

    def place_copy(slot):
        return pltpu.make_async_remote_copy(
            src_ref=own_place,
            dst_ref=source_place.at[slot],
            send_sem=place_send.at[slot],
            recv_sem=place_recv.at[slot],
            device_id=source_peer(slot),
            device_id_type=MESH,
        )

    def target_copy(block):
        return pltpu.make_async_remote_copy(
            src_ref=own_place,
            dst_ref=target_place.at[block],
            send_sem=target_send.at[block],
            recv_sem=target_recv.at[block],
            device_id=target_peer(block, -1),
            device_id_type=MESH,
        )

    def density_copy(sweep, slot):
        return pltpu.make_async_remote_copy(
            src_ref=density.at[sweep, 0],
            dst_ref=density.at[sweep, slot],
            send_sem=density_send.at[sweep, slot],
            recv_sem=density_recv.at[sweep, slot],
            device_id=source_peer(slot),
            device_id_type=MESH,
        )

    def partial_copy(sweep, block):
        return pltpu.make_async_remote_copy(
            src_ref=partial.at[sweep, block],
            dst_ref=arrived.at[sweep, block],
            send_sem=partial_send.at[sweep, block],
            recv_sem=partial_recv.at[sweep, block],
            device_id=target_peer(block),
            device_id_type=MESH,
        )

    def beside_copy(block):
        return pltpu.make_async_remote_copy(
            src_ref=partial.at[SWEEPS - 1, block],
            dst_ref=beside.at[block],
            send_sem=beside_send.at[block],
            recv_sem=beside_recv.at[block],
            device_id=beside_peer(block),
            device_id_type=MESH,
        )

    def fem_copy():
        return pltpu.make_async_remote_copy(
            src_ref=fem.at[0],
            dst_ref=fem.at[1],
            send_sem=fem_send,
            recv_sem=fem_recv,
            device_id=beside_peer(BLOCKS - 1),
            device_id_type=MESH,
        )

    def send_density(sweep, values):
        density[sweep, 0] = jnp.concatenate(
            [values[0], values[1], values[2], values[0]], axis=0
        ).astype(BF16)

        def start():
            for slot in reversed(range(1, SLOTS)):
                density_copy(sweep, slot).start()

        return start

    def widen(slot):
        values = source_place[slot]
        first = values.astype(BF16).astype(F32)
        rest = values - first
        second = rest.astype(BF16).astype(F32)
        third = rest - second
        parts = jnp.concatenate([first, second, third, jnp.zeros_like(third)], axis=0)
        wide = lax.dot_general(
            parts.astype(BF16),
            repeat[...],
            (((0,), (0,)), ((), ())),
            preferred_element_type=F32,
        )
        place = pl.ds(pl.multiple_of(slot * OWN, OWN), OWN)
        for i in range(5):
            source_wide[i, place, :] = wide[:, i * 128 : (i + 1) * 128]

    def tile_piece(pair, chunk):
        for block in (2 * pair, 2 * pair + 1):
            target = [
                jnp.broadcast_to(target_place[block, i : i + 1, :], (16, OWN)) for i in range(3)
            ]

            for step in range(16):
                place = pl.ds(pl.multiple_of(chunk * 256 + step * 16, 16), 16)
                source = [source_wide[i, place, :] for i in range(5)]
                values = kelvin_components(source, target)
                for k in range(COMPONENTS):
                    tile[k, block, place, :] = values[k].astype(BF16)

    def product(sweep, blocks, chunk, chunks):
        slots = range(2 * chunks)
        xy = jnp.concatenate([density[sweep, 2 * chunk + i, 0:16, :] for i in slots], axis=1)
        zx = jnp.concatenate([density[sweep, 2 * chunk + i, 16:32, :] for i in slots], axis=1)
        xyz = jnp.concatenate([xy, zx], axis=0)
        place = pl.ds(pl.multiple_of(chunk * 256, 256), chunks * 256)

        def dot(left, k):
            right = jnp.concatenate([tile[k, block, place, :] for block in blocks], axis=1)
            return jnp.dot(left, right, preferred_element_type=F32)

        p_xx = dot(xy, 0)
        p_xy = dot(xy, 1)
        p_xz = dot(zx, 2)
        p_yy = dot(xy, 3)
        p_yz = dot(xyz, 4)
        p_zz = dot(zx, 5)
        return (
            p_xx[0:8] + p_xy[8:16] + p_xz[0:8],
            p_xy[0:8] + p_yy[8:16] + p_yz[16:24],
            p_xz[8:16] + p_yz[8:16] + p_zz[0:8],
        )

    def accumulate(sweep, blocks, sums, first):
        for part, block in enumerate(blocks):
            for i in range(3):
                value = sums[i][:, part * OWN : (part + 1) * OWN]
                if not first:
                    value = value + partial[sweep, block, i]
                partial[sweep, block, i] = value

    def send_partial(sweep, blocks):
        for block in blocks:
            if block < BLOCKS - 1:
                partial_copy(sweep, block).start()

    def total_of(sweep):
        total = [partial[sweep, BLOCKS - 1, i] for i in range(3)]
        for block in reversed(range(BLOCKS - 1)):
            partial_copy(sweep, block).wait_recv()
            for i in range(3):
                total[i] = total[i] + arrived[sweep, block, i]
        return total

    stiffness = stiffness_ref[pl.ds(half, 1), :]

    def next_density(sweep):
        total = total_of(sweep)
        send_density(sweep + 1, [trac[i] - stiffness * total[i] for i in range(3)])()

    brick_side(
        (
            nodal,
            connect,
            size_ref,
            shear_ref,
            bulk_ref,
            cohesion_ref,
            friction_ref,
            active_ref,
            brick_ref,
            face_ref,
        ),
        half,
        trac,
        fem,
    )
    start_density = send_density(0, [trac[i] for i in range(3)])
    widen(0)

    pl.semaphore_wait(barrier, SLOTS - 1 + 2 * (BLOCKS - 1))

    for slot in range(1, 2 * NEAR):
        place_copy(slot).start()
    for block in range(BLOCKS - 1):
        target_copy(block).start()
    for slot in reversed(range(2 * NEAR, SLOTS)):
        place_copy(slot).start()
    start_density()
    fem_copy().start()

    for slot in range(1, 2 * NEAR):
        place_copy(slot).wait_recv()

    for slot in range(1, 2 * NEAR):
        widen(slot)

    for pair in reversed(range(PAIRS)):
        for block in (2 * pair, 2 * pair + 1):
            if block < BLOCKS - 1:
                target_copy(block).wait_recv()

        @pl.loop(0, NEAR)
        def _(chunk):
            tile_piece(pair, chunk)

    for slot in range(2 * NEAR, SLOTS):
        place_copy(slot).wait_recv()

    @pl.loop(2 * NEAR, SLOTS, step=6)
    def _(slot):
        for i in range(6):
            widen(slot + i)

    for slot in range(1, SLOTS):
        density_copy(0, slot).wait_recv()

    for pair in range(PAIRS):

        @pl.loop(NEAR, CHUNKS)
        def _(chunk):
            tile_piece(pair, chunk)

        blocks = (2 * pair, 2 * pair + 1)
        accumulate(0, blocks, product(0, blocks, 0, CHUNKS), True)
        send_partial(0, blocks)

    next_density(0)

    @pl.loop(1, SWEEPS)
    def _(sweep):
        for first, chunks in GROUPS:
            for slot in range(max(1, 2 * first), 2 * (first + chunks)):
                density_copy(sweep, slot).wait_recv()
            if first + chunks < CHUNKS:
                every = range(BLOCKS)
                accumulate(sweep, every, product(sweep, every, first, chunks), first == 0)
            else:
                for pair in range(PAIRS):
                    blocks = (2 * pair, 2 * pair + 1)
                    accumulate(sweep, blocks, product(sweep, blocks, first, chunks), False)

                    @pl.when(sweep == SWEEPS - 1)
                    def _():
                        for block in blocks:
                            beside_copy(block).start()

                    send_partial(sweep, blocks)

        @pl.when(sweep < SWEEPS - 1)
        def _():
            next_density(sweep)

    for slot in range(1, SLOTS):
        place_copy(slot).wait_send()
    for block in range(BLOCKS - 1):
        target_copy(block).wait_send()
    fem_copy().wait()

    @pl.loop(0, SWEEPS)
    def _(sweep):
        for slot in range(1, SLOTS):
            density_copy(sweep, slot).wait_send()
        for block in range(BLOCKS - 1):
            partial_copy(sweep, block).wait_send()

    own_total = total_of(SWEEPS - 1)
    for block in range(BLOCKS):
        beside_copy(block).wait_send()
    other_total = [jnp.zeros((8, OWN), F32)] * 3
    for block in reversed(range(BLOCKS)):
        beside_copy(block).wait_recv()
        for i in range(3):
            other_total[i] = other_total[i] + beside[block, i]
    for i in range(3):
        own_out = fem[0, i] + RELAXATION * (own_total[i] - fem[0, i])
        other_out = fem[1, i] + RELAXATION * (other_total[i] - fem[1, i])
        low = jnp.where(half == 0, own_out, other_out)
        high = jnp.where(half == 0, other_out, own_out)
        out_ref[i] = jnp.concatenate([low, high], axis=1)


def on_device(
    nodal_disp,
    connect,
    brick_size,
    shear_modulus,
    bulk_modulus,
    cohesion,
    friction,
    active,
    patch_brick,
    patch_face,
    coords,
    radius,
    stiffness,
):
    batches = nodal_disp.shape[0]
    local_nodes = coords.shape[1]
    anywhere = pl.BlockSpec(memory_space=pl.ANY)
    vmem = pl.BlockSpec(memory_space=pltpu.VMEM)
    dma = pltpu.SemaphoreType.DMA
    by_brick = [
        values.reshape(-1, 128)
        for values in (brick_size, shear_modulus, bulk_modulus, cohesion, friction, active)
    ]
    by_node = [values.reshape(-1, OWN) for values in (patch_brick, patch_face)]
    inputs = (
        nodal_disp.transpose(1, 0, 2),
        connect,
        *by_brick,
        *by_node,
        coords,
        radius.reshape(-1, OWN),
        stiffness.reshape(-1, OWN),
    )
    relaxed = pl.pallas_call(
        kernel,
        out_shape=jax.ShapeDtypeStruct((3, batches, local_nodes), F32),
        in_specs=[anywhere] * len(inputs),
        out_specs=vmem,
        scratch_shapes=[
            *(pltpu.VMEM(values.shape, values.dtype) for values in inputs),
            pltpu.VMEM((8, OWN), F32),
            pltpu.VMEM((SLOTS, 8, OWN), F32),
            pltpu.VMEM((BLOCKS, 8, OWN), F32),
            pltpu.VMEM((5, SOURCES, 128), F32),
            pltpu.VMEM((COMPONENTS, BLOCKS, SOURCES, 128), BF16),
            pltpu.VMEM((SWEEPS, SLOTS, 32, OWN), BF16),
            pltpu.VMEM((SWEEPS, BLOCKS, 3, 8, OWN), F32),
            pltpu.VMEM((SWEEPS, BLOCKS, 3, 8, OWN), F32),
            pltpu.VMEM((3, 8, OWN), F32),
            pltpu.VMEM((2, 3, 8, OWN), F32),
            pltpu.VMEM((BLOCKS, 3, 8, OWN), F32),
            pltpu.VMEM((32, 5 * 128), BF16),
            dma((len(inputs),)),
            dma((SLOTS,)),
            dma((SLOTS,)),
            dma((BLOCKS,)),
            dma((BLOCKS,)),
            dma((SWEEPS, SLOTS)),
            dma((SWEEPS, SLOTS)),
            dma((SWEEPS, BLOCKS)),
            dma((SWEEPS, BLOCKS)),
            dma((BLOCKS,)),
            dma((BLOCKS,)),
            dma,
            dma,
        ],
        compiler_params=pltpu.CompilerParams(
            collective_id=0, has_side_effects=True, vmem_limit_bytes=60 * 2**20
        ),
    )(
        *inputs
    )
    return relaxed.transpose(1, 0, 2)


def solution(mesh):
    split = ("blk", "rows")
    return jax.shard_map(
        on_device,
        mesh=mesh,
        in_specs=(
            P(None, None, split),
            P(None, split),
            P(split),
            P(split),
            P(split),
            P(split),
            P(split),
            P(split),
            P(split),
            P(split),
            P(None, split),
            P(split),
            P(split),
        ),
        out_specs=P(None, None, split),
        check_vma=False,
    )
```

```python
import math

import jax
import jax.numpy as jnp
from jax import lax
from jax.experimental import pallas as pl
from jax.experimental.pallas import tpu as pltpu
from jax.sharding import PartitionSpec as P

SWEEPS = 3

KELVIN_A = 1.0 / (1024.0 * math.pi)
KELVIN_B = KELVIN_A / 3.0
SMOOTH = 0.1
RELAXATION = 0.5

F32 = jnp.float32
BF16 = jnp.bfloat16
MESH = pl.DeviceIdType.MESH
OWN = 128


def hops(step):
    return min(step % 4, 4 - step % 4)


SOURCE_STEPS = sorted(
    ((dz, dy) for dz in range(4) for dy in range(4)),
    key=lambda step: (hops(step[0]) + hops(step[1]), step),
)
TARGET_STEPS = [(2, 0), (2, 1), (1, 0), (1, 1), (3, 0), (3, 1), (0, 1), (0, 0)]
SLOTS = len(SOURCE_STEPS)
BLOCKS = len(TARGET_STEPS)
SOURCES = SLOTS * OWN
PAIRS = BLOCKS // 2
CHUNKS = SLOTS // 2
NEAR = 2
EARLY = 2
COMPONENTS = 6


def lane_gather(values, index):
    numbers = lax.GatherDimensionNumbers(
        offset_dims=(),
        collapsed_slice_dims=(1,),
        start_index_map=(1,),
        operand_batching_dims=(0,),
        start_indices_batching_dims=(0,),
    )
    return lax.gather(
        values,
        index[:, :, None],
        numbers,
        (1, 1),
        mode=lax.GatherScatterMode.PROMISE_IN_BOUNDS,
    )


def brick_side(refs, half, trac_ref, fem_ref):
    nodal, connect, size, shear, bulk, cohesion, friction, active, brick, face = refs
    node_brick = brick[pl.ds(half, 1), :]
    node_face = face[pl.ds(half, 1), :]
    high = jnp.broadcast_to(node_brick // 128, (8, OWN))
    low = jnp.broadcast_to(node_brick % 128, (8, OWN))

    def pick_corner(tile, corners):
        part = connect[:, pl.ds(pl.multiple_of(tile * 128, 128), 128)]
        return jnp.where(high == tile, lane_gather(part, low), corners)

    corners = lax.fori_loop(0, 32, pick_corner, jnp.zeros((8, OWN), jnp.int32), unroll=16)
    row = lax.broadcasted_iota(jnp.int32, (8, OWN), 0)

    def pick(values):
        total = jnp.zeros((8, OWN), F32)
        for group in range(4):
            part = lane_gather(values[8 * group : 8 * group + 8], low)
            total = total + jnp.where(high == row + 8 * group, part, 0.0)
        return jnp.sum(total, axis=0, keepdims=True)

    size_at = pick(size[...])
    shear_at = pick(shear[...])
    bulk_at = pick(bulk[...])
    cohesion_at = pick(cohesion[...])
    friction_at = pick(friction[...])
    active_at = pick(jnp.where(active[...] == 1, 1.0, 0.0))

    corner_high = [jnp.broadcast_to(corners[c : c + 1] // 128, (8, OWN)) for c in range(8)]
    corner_low = [jnp.broadcast_to(corners[c : c + 1] % 128, (8, OWN)) for c in range(8)]

    zero = jnp.zeros((8, OWN), F32)
    picked = []
    for c in range(8):

        def pick_nodes(tile, values, c=c):
            columns = pl.ds(pl.multiple_of(tile * 128, 128), 128)
            here = corner_high[c] == tile
            return tuple(
                jnp.where(here, lane_gather(nodal[i, :, columns], corner_low[c]), values[i])
                for i in range(3)
            )

        picked.extend(lax.fori_loop(0, 32, pick_nodes, (zero,) * 3, unroll=16))

    gradient = [[zero] * 3 for _ in range(3)]
    centre = [zero] * 3
    for c in range(8):
        for i in range(3):
            value = picked[3 * c + i]
            centre[i] = centre[i] + value
            for j in range(3):
                if (c >> j) & 1:
                    gradient[i][j] = gradient[i][j] + value
                else:
                    gradient[i][j] = gradient[i][j] - value
    divisor = 4.0 * size_at
    gradient = [[g / divisor for g in line] for line in gradient]
    centre = [value / 8.0 for value in centre]
    strain = [[0.5 * (gradient[i][j] + gradient[j][i]) for j in range(3)] for i in range(3)]
    volume = strain[0][0] + strain[1][1] + strain[2][2]
    pressure = bulk_at * volume
    third = volume / 3.0
    deviator = [
        [2.0 * shear_at * (strain[i][j] - (third if i == j else 0.0)) for j in range(3)]
        for i in range(3)
    ]
    second = zero
    for i in range(3):
        for j in range(3):
            second = second + deviator[i][j] * deviator[i][j]
    second = 0.5 * second
    scaling = jnp.maximum(cohesion_at - friction_at * pressure, SMOOTH) / jnp.sqrt(
        second + SMOOTH * SMOOTH
    )
    scaling = jnp.where(active_at == 1.0, scaling, 1.0)
    axis_of = node_face // 2
    sign = (1 - 2 * (node_face % 2)).astype(F32)
    for i in range(3):
        line = [scaling * deviator[i][k] + (pressure if i == k else 0.0) for k in range(3)]
        chosen = jnp.where(axis_of == 0, line[0], jnp.where(axis_of == 1, line[1], line[2]))
        trac_ref[i] = (chosen * sign).astype(BF16).astype(F32)
        fem_ref[0, i] = centre[i].astype(BF16).astype(F32)


def kelvin_components(source, target):
    sx, sy, sz, spread, spread_more = source
    dx, dy, dz = target[0] - sx, target[1] - sy, target[2] - sz
    xx, yy, zz = dx * dx, dy * dy, dz * dz
    squared = ((xx + yy) + zz) + spread
    common = squared + (squared + spread_more)
    inverse = lax.rsqrt(squared)
    weight = (inverse * inverse) * (inverse * KELVIN_B)
    wx, wy = weight * dx, weight * dy
    return (
        weight * (xx + common),
        wx * dy,
        wx * dz,
        weight * (yy + common),
        wy * dz,
        weight * (zz + common),
    )


def kernel(
    nodal_hbm,
    connect_hbm,
    size_hbm,
    shear_hbm,
    bulk_hbm,
    cohesion_hbm,
    friction_hbm,
    active_hbm,
    brick_hbm,
    face_hbm,
    coords_hbm,
    radius_hbm,
    stiffness_hbm,
    out_ref,
    nodal,
    connect,
    size_ref,
    shear_ref,
    bulk_ref,
    cohesion_ref,
    friction_ref,
    active_ref,
    brick_ref,
    face_ref,
    coords_ref,
    radius_ref,
    stiffness_ref,
    own_place,
    source_place,
    target_place,
    source_wide,
    tile,
    density,
    partial,
    arrived,
    trac,
    fem,
    beside,
    repeat,
    local_sem,
    place_send,
    place_recv,
    target_send,
    target_recv,
    density_send,
    density_recv,
    partial_send,
    partial_recv,
    beside_send,
    beside_recv,
    fem_send,
    fem_recv,
):
    half = lax.axis_index("segment")
    blk = lax.axis_index("blk")
    rows = lax.axis_index("rows")
    z, y = blk // 2, (blk % 2) * 2 + half
    x, core = rows // 2, rows % 2

    def source_peer(slot):
        dz, dy = SOURCE_STEPS[slot]
        pz, py = (z + dz) % 4, (y + dy) % 4
        return (py % 2, pz * 2 + py // 2, rows)

    def target_peer(block, sign=1):
        dx, dc = TARGET_STEPS[block]
        px, pc = (x + 4 + sign * dx) % 4, (core + dc) % 2
        return (half, blk, px * 2 + pc)

    def beside_peer(block):
        _, _, peer_rows = target_peer(block)
        return ((half + 1) % 2, blk, peer_rows)

    barrier = pltpu.get_barrier_semaphore()
    peers = [source_peer(slot) for slot in reversed(range(1, SLOTS))]
    peers[5:5] = [beside_peer(block) for block in range(BLOCKS - 1)]
    peers += [target_peer(block) for block in range(BLOCKS - 1)]
    for peer in peers:
        pl.semaphore_signal(barrier, inc=1, device_id=peer, device_id_type=MESH)

    place_loads = [(coords_hbm, coords_ref), (radius_hbm, radius_ref)]
    brick_loads = [
        (brick_hbm, brick_ref),
        (connect_hbm, connect),
        (nodal_hbm, nodal),
        (face_hbm, face_ref),
        (size_hbm, size_ref),
        (shear_hbm, shear_ref),
        (bulk_hbm, bulk_ref),
        (cohesion_hbm, cohesion_ref),
        (friction_hbm, friction_ref),
        (active_hbm, active_ref),
        (stiffness_hbm, stiffness_ref),
    ]
    loads = [
        pltpu.make_async_copy(source, target, local_sem.at[i])
        for i, (source, target) in enumerate(place_loads + brick_loads)
    ]
    for load in loads:
        load.start()

    for load in loads[: len(place_loads)]:
        load.wait()
    own = pl.ds(pl.multiple_of(half * OWN, OWN), OWN)
    radius = radius_ref[pl.ds(half, 1), :]
    own_place[0:3, :] = coords_ref[:, own]
    own_place[3:4, :] = radius * radius
    own_place[4:5, :] = 1.5 * (radius * radius)
    own_place[5:8, :] = jnp.zeros((3, OWN), F32)
    row = lax.broadcasted_iota(jnp.int32, repeat.shape, 0)
    column = lax.broadcasted_iota(jnp.int32, repeat.shape, 1)
    repeat[...] = jnp.where((row % 8 == column // 128) & (row < 24), 1.0, 0.0).astype(BF16)
    source_place[0] = own_place[...]
    target_place[BLOCKS - 1] = own_place[...]

    for load in loads[len(place_loads) :]:
        load.wait()

    def place_copy(slot):
        return pltpu.make_async_remote_copy(
            src_ref=own_place,
            dst_ref=source_place.at[slot],
            send_sem=place_send.at[slot],
            recv_sem=place_recv.at[slot],
            device_id=source_peer(slot),
            device_id_type=MESH,
        )

    def target_copy(block):
        return pltpu.make_async_remote_copy(
            src_ref=own_place,
            dst_ref=target_place.at[block],
            send_sem=target_send.at[block],
            recv_sem=target_recv.at[block],
            device_id=target_peer(block, -1),
            device_id_type=MESH,
        )

    def density_copy(sweep, slot):
        return pltpu.make_async_remote_copy(
            src_ref=density.at[sweep, 0],
            dst_ref=density.at[sweep, slot],
            send_sem=density_send.at[sweep, slot],
            recv_sem=density_recv.at[sweep, slot],
            device_id=source_peer(slot),
            device_id_type=MESH,
        )

    def partial_copy(sweep, block):
        return pltpu.make_async_remote_copy(
            src_ref=partial.at[sweep, block],
            dst_ref=arrived.at[sweep, block],
            send_sem=partial_send.at[sweep, block],
            recv_sem=partial_recv.at[sweep, block],
            device_id=target_peer(block),
            device_id_type=MESH,
        )

    def beside_copy(block):
        return pltpu.make_async_remote_copy(
            src_ref=partial.at[SWEEPS - 1, block],
            dst_ref=beside.at[block],
            send_sem=beside_send.at[block],
            recv_sem=beside_recv.at[block],
            device_id=beside_peer(block),
            device_id_type=MESH,
        )

    def fem_copy():
        return pltpu.make_async_remote_copy(
            src_ref=fem.at[0],
            dst_ref=fem.at[1],
            send_sem=fem_send,
            recv_sem=fem_recv,
            device_id=beside_peer(BLOCKS - 1),
            device_id_type=MESH,
        )

    def send_density(sweep, values):
        density[sweep, 0] = jnp.concatenate(
            [values[0], values[1], values[2], values[0]], axis=0
        ).astype(BF16)

        def start():
            for slot in reversed(range(1, SLOTS)):
                density_copy(sweep, slot).start()

        return start

    def widen(slot):
        values = source_place[slot]
        first = values.astype(BF16).astype(F32)
        rest = values - first
        second = rest.astype(BF16).astype(F32)
        third = rest - second
        parts = jnp.concatenate([first, second, third, jnp.zeros_like(third)], axis=0)
        wide = lax.dot_general(
            parts.astype(BF16),
            repeat[...],
            (((0,), (0,)), ((), ())),
            preferred_element_type=F32,
        )
        place = pl.ds(pl.multiple_of(slot * OWN, OWN), OWN)
        for i in range(5):
            source_wide[i, place, :] = wide[:, i * 128 : (i + 1) * 128]

    def tile_piece(pair, chunk):
        for block in (2 * pair, 2 * pair + 1):
            target = [
                jnp.broadcast_to(target_place[block, i : i + 1, :], (16, OWN)) for i in range(3)
            ]

            for step in range(16):
                place = pl.ds(pl.multiple_of(chunk * 256 + step * 16, 16), 16)
                source = [source_wide[i, place, :] for i in range(5)]
                values = kelvin_components(source, target)
                for k in range(COMPONENTS):
                    tile[k, block, place, :] = values[k].astype(BF16)

    def product(sweep, blocks, chunk, chunks):
        slots = range(2 * chunks)
        xy = jnp.concatenate([density[sweep, 2 * chunk + i, 0:16, :] for i in slots], axis=1)
        zx = jnp.concatenate([density[sweep, 2 * chunk + i, 16:32, :] for i in slots], axis=1)
        xyz = jnp.concatenate([xy, zx], axis=0)
        place = pl.ds(pl.multiple_of(chunk * 256, 256), chunks * 256)

        def dot(left, k):
            right = jnp.concatenate([tile[k, block, place, :] for block in blocks], axis=1)
            return jnp.dot(left, right, preferred_element_type=F32)

        p_xx = dot(xy, 0)
        p_xy = dot(xy, 1)
        p_xz = dot(zx, 2)
        p_yy = dot(xy, 3)
        p_yz = dot(xyz, 4)
        p_zz = dot(zx, 5)
        return (
            p_xx[0:8] + p_xy[8:16] + p_xz[0:8],
            p_xy[0:8] + p_yy[8:16] + p_yz[16:24],
            p_xz[8:16] + p_yz[8:16] + p_zz[0:8],
        )

    def accumulate(sweep, blocks, sums, first):
        for part, block in enumerate(blocks):
            for i in range(3):
                value = sums[i][:, part * OWN : (part + 1) * OWN]
                if not first:
                    value = value + partial[sweep, block, i]
                partial[sweep, block, i] = value

    def send_partial(sweep, blocks):
        for block in blocks:
            if block < BLOCKS - 1:
                partial_copy(sweep, block).start()

    def total_of(sweep):
        total = [partial[sweep, BLOCKS - 1, i] for i in range(3)]
        for block in reversed(range(BLOCKS - 1)):
            partial_copy(sweep, block).wait_recv()
            for i in range(3):
                total[i] = total[i] + arrived[sweep, block, i]
        return total

    stiffness = stiffness_ref[pl.ds(half, 1), :]

    def next_density(sweep):
        total = total_of(sweep)
        send_density(sweep + 1, [trac[i] - stiffness * total[i] for i in range(3)])()

    brick_side(
        (
            nodal,
            connect,
            size_ref,
            shear_ref,
            bulk_ref,
            cohesion_ref,
            friction_ref,
            active_ref,
            brick_ref,
            face_ref,
        ),
        half,
        trac,
        fem,
    )
    start_density = send_density(0, [trac[i] for i in range(3)])
    widen(0)

    pl.semaphore_wait(barrier, SLOTS - 1 + 2 * (BLOCKS - 1))

    for slot in range(1, 2 * NEAR):
        place_copy(slot).start()
    for block in range(BLOCKS - 1):
        target_copy(block).start()
    for slot in reversed(range(2 * NEAR, SLOTS)):
        place_copy(slot).start()
    start_density()
    fem_copy().start()

    for slot in range(1, 2 * NEAR):
        place_copy(slot).wait_recv()

    for slot in range(1, 2 * NEAR):
        widen(slot)

    for pair in reversed(range(PAIRS)):
        for block in (2 * pair, 2 * pair + 1):
            if block < BLOCKS - 1:
                target_copy(block).wait_recv()

        @pl.loop(0, NEAR)
        def _(chunk):
            tile_piece(pair, chunk)

    for slot in range(2 * NEAR, SLOTS):
        place_copy(slot).wait_recv()

    @pl.loop(2 * NEAR, SLOTS, step=6)
    def _(slot):
        for i in range(6):
            widen(slot + i)

    for slot in range(1, SLOTS):
        density_copy(0, slot).wait_recv()

    for pair in range(PAIRS):

        @pl.loop(NEAR, CHUNKS)
        def _(chunk):
            tile_piece(pair, chunk)

        blocks = (2 * pair, 2 * pair + 1)
        accumulate(0, blocks, product(0, blocks, 0, CHUNKS), True)
        send_partial(0, blocks)

    next_density(0)

    @pl.loop(1, SWEEPS)
    def _(sweep):
        remote, near_pair = range(BLOCKS - 2), range(BLOCKS - 2, BLOCKS)
        for slot in range(1, 2 * EARLY):
            density_copy(sweep, slot).wait_recv()
        accumulate(sweep, remote, product(sweep, remote, 0, EARLY), True)
        for slot in range(2 * EARLY, SLOTS):
            density_copy(sweep, slot).wait_recv()
        for pair in range(PAIRS):
            blocks = (2 * pair, 2 * pair + 1)
            if pair < PAIRS - 1:
                sums = product(sweep, blocks, EARLY, CHUNKS - EARLY)
                accumulate(sweep, blocks, sums, False)
            else:
                accumulate(sweep, blocks, product(sweep, blocks, 0, CHUNKS), True)

            @pl.when(sweep == SWEEPS - 1)
            def _():
                for block in blocks:
                    beside_copy(block).start()

            send_partial(sweep, blocks)

        @pl.when(sweep < SWEEPS - 1)
        def _():
            next_density(sweep)

    for slot in range(1, SLOTS):
        place_copy(slot).wait_send()
    for block in range(BLOCKS - 1):
        target_copy(block).wait_send()
    fem_copy().wait()

    @pl.loop(0, SWEEPS)
    def _(sweep):
        for slot in range(1, SLOTS):
            density_copy(sweep, slot).wait_send()
        for block in range(BLOCKS - 1):
            partial_copy(sweep, block).wait_send()

    own_total = total_of(SWEEPS - 1)
    for block in range(BLOCKS):
        beside_copy(block).wait_send()
    other_total = [jnp.zeros((8, OWN), F32)] * 3
    for block in reversed(range(BLOCKS)):
        beside_copy(block).wait_recv()
        for i in range(3):
            other_total[i] = other_total[i] + beside[block, i]
    for i in range(3):
        own_out = fem[0, i] + RELAXATION * (own_total[i] - fem[0, i])
        other_out = fem[1, i] + RELAXATION * (other_total[i] - fem[1, i])
        low = jnp.where(half == 0, own_out, other_out)
        high = jnp.where(half == 0, other_out, own_out)
        out_ref[i] = jnp.concatenate([low, high], axis=1)


def on_device(
    nodal_disp,
    connect,
    brick_size,
    shear_modulus,
    bulk_modulus,
    cohesion,
    friction,
    active,
    patch_brick,
    patch_face,
    coords,
    radius,
    stiffness,
):
    batches = nodal_disp.shape[0]
    local_nodes = coords.shape[1]
    anywhere = pl.BlockSpec(memory_space=pl.ANY)
    vmem = pl.BlockSpec(memory_space=pltpu.VMEM)
    dma = pltpu.SemaphoreType.DMA
    by_brick = [
        values.reshape(-1, 128)
        for values in (brick_size, shear_modulus, bulk_modulus, cohesion, friction, active)
    ]
    by_node = [values.reshape(-1, OWN) for values in (patch_brick, patch_face)]
    inputs = (
        nodal_disp.transpose(1, 0, 2),
        connect,
        *by_brick,
        *by_node,
        coords,
        radius.reshape(-1, OWN),
        stiffness.reshape(-1, OWN),
    )
    relaxed = pl.pallas_call(
        kernel,
        out_shape=jax.ShapeDtypeStruct((3, batches, local_nodes), F32),
        in_specs=[anywhere] * len(inputs),
        out_specs=vmem,
        scratch_shapes=[
            *(pltpu.VMEM(values.shape, values.dtype) for values in inputs),
            pltpu.VMEM((8, OWN), F32),
            pltpu.VMEM((SLOTS, 8, OWN), F32),
            pltpu.VMEM((BLOCKS, 8, OWN), F32),
            pltpu.VMEM((5, SOURCES, 128), F32),
            pltpu.VMEM((COMPONENTS, BLOCKS, SOURCES, 128), BF16),
            pltpu.VMEM((SWEEPS, SLOTS, 32, OWN), BF16),
            pltpu.VMEM((SWEEPS, BLOCKS, 3, 8, OWN), F32),
            pltpu.VMEM((SWEEPS, BLOCKS, 3, 8, OWN), F32),
            pltpu.VMEM((3, 8, OWN), F32),
            pltpu.VMEM((2, 3, 8, OWN), F32),
            pltpu.VMEM((BLOCKS, 3, 8, OWN), F32),
            pltpu.VMEM((32, 5 * 128), BF16),
            dma((len(inputs),)),
            dma((SLOTS,)),
            dma((SLOTS,)),
            dma((BLOCKS,)),
            dma((BLOCKS,)),
            dma((SWEEPS, SLOTS)),
            dma((SWEEPS, SLOTS)),
            dma((SWEEPS, BLOCKS)),
            dma((SWEEPS, BLOCKS)),
            dma((BLOCKS,)),
            dma((BLOCKS,)),
            dma,
            dma,
        ],
        compiler_params=pltpu.CompilerParams(
            collective_id=0, has_side_effects=True, vmem_limit_bytes=60 * 2**20
        ),
    )(
        *inputs
    )
    return relaxed.transpose(1, 0, 2)


def solution(mesh):
    split = ("blk", "rows")
    return jax.shard_map(
        on_device,
        mesh=mesh,
        in_specs=(
            P(None, None, split),
            P(None, split),
            P(split),
            P(split),
            P(split),
            P(split),
            P(split),
            P(split),
            P(split),
            P(split),
            P(None, split),
            P(split),
            P(split),
        ),
        out_specs=P(None, None, split),
        check_vma=False,
    )
```

```python
import math

import jax
import jax.numpy as jnp
from jax import lax
from jax.experimental import pallas as pl
from jax.experimental.pallas import tpu as pltpu
from jax.sharding import PartitionSpec as P

SWEEPS = 3

KELVIN_A = 1.0 / (1024.0 * math.pi)
KELVIN_B = KELVIN_A / 3.0
SMOOTH = 0.1
RELAXATION = 0.5

F32 = jnp.float32
BF16 = jnp.bfloat16
MESH = pl.DeviceIdType.MESH
OWN = 128


def hops(step):
    return min(step % 4, 4 - step % 4)


SOURCE_STEPS = sorted(
    ((dz, dy) for dz in range(4) for dy in range(4)),
    key=lambda step: (hops(step[0]) + hops(step[1]), step),
)
TARGET_STEPS = [(2, 0), (2, 1), (1, 0), (1, 1), (3, 0), (3, 1), (0, 1), (0, 0)]
SLOTS = len(SOURCE_STEPS)
BLOCKS = len(TARGET_STEPS)
SOURCES = SLOTS * OWN
PAIRS = BLOCKS // 2
CHUNKS = SLOTS // 2
NEAR = 2
EARLY = 2
COMPONENTS = 6


def lane_gather(values, index):
    numbers = lax.GatherDimensionNumbers(
        offset_dims=(),
        collapsed_slice_dims=(1,),
        start_index_map=(1,),
        operand_batching_dims=(0,),
        start_indices_batching_dims=(0,),
    )
    return lax.gather(
        values,
        index[:, :, None],
        numbers,
        (1, 1),
        mode=lax.GatherScatterMode.PROMISE_IN_BOUNDS,
    )


def brick_side(refs, half, trac_ref, fem_ref):
    nodal, connect, size, shear, bulk, cohesion, friction, active, brick, face = refs
    node_brick = brick[pl.ds(half, 1), :]
    node_face = face[pl.ds(half, 1), :]
    high = jnp.broadcast_to(node_brick // 128, (8, OWN))
    low = jnp.broadcast_to(node_brick % 128, (8, OWN))

    def pick_corner(tile, corners):
        part = connect[:, pl.ds(pl.multiple_of(tile * 128, 128), 128)]
        return jnp.where(high == tile, lane_gather(part, low), corners)

    corners = lax.fori_loop(0, 32, pick_corner, jnp.zeros((8, OWN), jnp.int32), unroll=16)
    row = lax.broadcasted_iota(jnp.int32, (8, OWN), 0)

    def pick(values):
        total = jnp.zeros((8, OWN), F32)
        for group in range(4):
            part = lane_gather(values[8 * group : 8 * group + 8], low)
            total = total + jnp.where(high == row + 8 * group, part, 0.0)
        return jnp.sum(total, axis=0, keepdims=True)

    size_at = pick(size[...])
    shear_at = pick(shear[...])
    bulk_at = pick(bulk[...])
    cohesion_at = pick(cohesion[...])
    friction_at = pick(friction[...])
    active_at = pick(jnp.where(active[...] == 1, 1.0, 0.0))

    corner_high = [jnp.broadcast_to(corners[c : c + 1] // 128, (8, OWN)) for c in range(8)]
    corner_low = [jnp.broadcast_to(corners[c : c + 1] % 128, (8, OWN)) for c in range(8)]

    zero = jnp.zeros((8, OWN), F32)
    picked = []
    for c in range(8):

        def pick_nodes(tile, values, c=c):
            columns = pl.ds(pl.multiple_of(tile * 128, 128), 128)
            here = corner_high[c] == tile
            return tuple(
                jnp.where(here, lane_gather(nodal[i, :, columns], corner_low[c]), values[i])
                for i in range(3)
            )

        picked.extend(lax.fori_loop(0, 32, pick_nodes, (zero,) * 3, unroll=16))

    gradient = [[zero] * 3 for _ in range(3)]
    centre = [zero] * 3
    for c in range(8):
        for i in range(3):
            value = picked[3 * c + i]
            centre[i] = centre[i] + value
            for j in range(3):
                if (c >> j) & 1:
                    gradient[i][j] = gradient[i][j] + value
                else:
                    gradient[i][j] = gradient[i][j] - value
    divisor = 4.0 * size_at
    gradient = [[g / divisor for g in line] for line in gradient]
    centre = [value / 8.0 for value in centre]
    strain = [[0.5 * (gradient[i][j] + gradient[j][i]) for j in range(3)] for i in range(3)]
    volume = strain[0][0] + strain[1][1] + strain[2][2]
    pressure = bulk_at * volume
    third = volume / 3.0
    deviator = [
        [2.0 * shear_at * (strain[i][j] - (third if i == j else 0.0)) for j in range(3)]
        for i in range(3)
    ]
    second = zero
    for i in range(3):
        for j in range(3):
            second = second + deviator[i][j] * deviator[i][j]
    second = 0.5 * second
    scaling = jnp.maximum(cohesion_at - friction_at * pressure, SMOOTH) / jnp.sqrt(
        second + SMOOTH * SMOOTH
    )
    scaling = jnp.where(active_at == 1.0, scaling, 1.0)
    axis_of = node_face // 2
    sign = (1 - 2 * (node_face % 2)).astype(F32)
    for i in range(3):
        line = [scaling * deviator[i][k] + (pressure if i == k else 0.0) for k in range(3)]
        chosen = jnp.where(axis_of == 0, line[0], jnp.where(axis_of == 1, line[1], line[2]))
        trac_ref[i] = (chosen * sign).astype(BF16).astype(F32)
        fem_ref[0, i] = centre[i].astype(BF16).astype(F32)


def kelvin_components(source, target):
    sx, sy, sz, spread, spread_more = source
    dx, dy, dz = target[0] - sx, target[1] - sy, target[2] - sz
    xx, yy, zz = dx * dx, dy * dy, dz * dz
    squared = ((xx + yy) + zz) + spread
    common = squared + (squared + spread_more)
    inverse = lax.rsqrt(squared)
    weight = (inverse * inverse) * (inverse * KELVIN_B)
    wx, wy = weight * dx, weight * dy
    return (
        weight * (xx + common),
        wx * dy,
        wx * dz,
        weight * (yy + common),
        wy * dz,
        weight * (zz + common),
    )


def kernel(
    nodal_hbm,
    connect_hbm,
    size_hbm,
    shear_hbm,
    bulk_hbm,
    cohesion_hbm,
    friction_hbm,
    active_hbm,
    brick_hbm,
    face_hbm,
    coords_hbm,
    radius_hbm,
    stiffness_hbm,
    out_ref,
    nodal,
    connect,
    size_ref,
    shear_ref,
    bulk_ref,
    cohesion_ref,
    friction_ref,
    active_ref,
    brick_ref,
    face_ref,
    coords_ref,
    radius_ref,
    stiffness_ref,
    own_place,
    source_place,
    target_place,
    source_wide,
    tile,
    density,
    partial,
    arrived,
    trac,
    fem,
    beside,
    repeat,
    local_sem,
    place_send,
    place_recv,
    target_send,
    target_recv,
    density_send,
    density_recv,
    partial_send,
    partial_recv,
    beside_send,
    beside_recv,
    fem_send,
    fem_recv,
):
    half = lax.axis_index("segment")
    blk = lax.axis_index("blk")
    rows = lax.axis_index("rows")
    z, y = blk // 2, (blk % 2) * 2 + half
    x, core = rows // 2, rows % 2

    def source_peer(slot):
        dz, dy = SOURCE_STEPS[slot]
        pz, py = (z + dz) % 4, (y + dy) % 4
        return (py % 2, pz * 2 + py // 2, rows)

    def target_peer(block, sign=1):
        dx, dc = TARGET_STEPS[block]
        px, pc = (x + 4 + sign * dx) % 4, (core + dc) % 2
        return (half, blk, px * 2 + pc)

    def beside_peer(block):
        _, _, peer_rows = target_peer(block)
        return ((half + 1) % 2, blk, peer_rows)

    barrier = pltpu.get_barrier_semaphore()
    peers = [source_peer(slot) for slot in reversed(range(1, SLOTS))]
    peers[5:5] = [beside_peer(block) for block in range(BLOCKS - 1)]
    peers += [target_peer(block) for block in range(BLOCKS - 1)]
    for peer in peers:
        pl.semaphore_signal(barrier, inc=1, device_id=peer, device_id_type=MESH)

    place_loads = [(coords_hbm, coords_ref), (radius_hbm, radius_ref)]
    brick_loads = [
        (brick_hbm, brick_ref),
        (connect_hbm, connect),
        (nodal_hbm, nodal),
        (face_hbm, face_ref),
        (size_hbm, size_ref),
        (shear_hbm, shear_ref),
        (bulk_hbm, bulk_ref),
        (cohesion_hbm, cohesion_ref),
        (friction_hbm, friction_ref),
        (active_hbm, active_ref),
        (stiffness_hbm, stiffness_ref),
    ]
    loads = [
        pltpu.make_async_copy(source, target, local_sem.at[i])
        for i, (source, target) in enumerate(place_loads + brick_loads)
    ]
    for load in loads:
        load.start()

    for load in loads[: len(place_loads)]:
        load.wait()
    own = pl.ds(pl.multiple_of(half * OWN, OWN), OWN)
    radius = radius_ref[pl.ds(half, 1), :]
    own_place[0:3, :] = coords_ref[:, own]
    own_place[3:4, :] = radius * radius
    own_place[4:5, :] = 1.5 * (radius * radius)
    own_place[5:8, :] = jnp.zeros((3, OWN), F32)
    row = lax.broadcasted_iota(jnp.int32, repeat.shape, 0)
    column = lax.broadcasted_iota(jnp.int32, repeat.shape, 1)
    repeat[...] = jnp.where((row % 8 == column // 128) & (row < 24), 1.0, 0.0).astype(BF16)
    source_place[0] = own_place[...]
    target_place[BLOCKS - 1] = own_place[...]

    for load in loads[len(place_loads) :]:
        load.wait()

    def place_copy(slot):
        return pltpu.make_async_remote_copy(
            src_ref=own_place,
            dst_ref=source_place.at[slot],
            send_sem=place_send.at[slot],
            recv_sem=place_recv.at[slot],
            device_id=source_peer(slot),
            device_id_type=MESH,
        )

    def target_copy(block):
        return pltpu.make_async_remote_copy(
            src_ref=own_place,
            dst_ref=target_place.at[block],
            send_sem=target_send.at[block],
            recv_sem=target_recv.at[block],
            device_id=target_peer(block, -1),
            device_id_type=MESH,
        )

    def density_copy(sweep, slot):
        return pltpu.make_async_remote_copy(
            src_ref=density.at[sweep, 0],
            dst_ref=density.at[sweep, slot],
            send_sem=density_send.at[sweep, slot],
            recv_sem=density_recv.at[sweep, slot],
            device_id=source_peer(slot),
            device_id_type=MESH,
        )

    def partial_copy(sweep, block):
        return pltpu.make_async_remote_copy(
            src_ref=partial.at[sweep, block],
            dst_ref=arrived.at[sweep, block],
            send_sem=partial_send.at[sweep, block],
            recv_sem=partial_recv.at[sweep, block],
            device_id=target_peer(block),
            device_id_type=MESH,
        )

    def beside_copy(block):
        return pltpu.make_async_remote_copy(
            src_ref=partial.at[SWEEPS - 1, block],
            dst_ref=beside.at[block],
            send_sem=beside_send.at[block],
            recv_sem=beside_recv.at[block],
            device_id=beside_peer(block),
            device_id_type=MESH,
        )

    def fem_copy():
        return pltpu.make_async_remote_copy(
            src_ref=fem.at[0],
            dst_ref=fem.at[1],
            send_sem=fem_send,
            recv_sem=fem_recv,
            device_id=beside_peer(BLOCKS - 1),
            device_id_type=MESH,
        )

    def send_density(sweep, values):
        density[sweep, 0] = jnp.concatenate(
            [values[0], values[1], values[2], values[0]], axis=0
        ).astype(BF16)

        def start():
            for slot in reversed(range(1, SLOTS)):
                density_copy(sweep, slot).start()

        return start

    def widen(slot):
        values = source_place[slot]
        first = values.astype(BF16).astype(F32)
        rest = values - first
        second = rest.astype(BF16).astype(F32)
        third = rest - second
        parts = jnp.concatenate([first, second, third, jnp.zeros_like(third)], axis=0)
        wide = lax.dot_general(
            parts.astype(BF16),
            repeat[...],
            (((0,), (0,)), ((), ())),
            preferred_element_type=F32,
        )
        place = pl.ds(pl.multiple_of(slot * OWN, OWN), OWN)
        for i in range(5):
            source_wide[i, place, :] = wide[:, i * 128 : (i + 1) * 128]

    def tile_piece(pair, chunk):
        for block in (2 * pair, 2 * pair + 1):
            target = [
                jnp.broadcast_to(target_place[block, i : i + 1, :], (16, OWN)) for i in range(3)
            ]

            for step in range(16):
                place = pl.ds(pl.multiple_of(chunk * 256 + step * 16, 16), 16)
                source = [source_wide[i, place, :] for i in range(5)]
                values = kelvin_components(source, target)
                for k in range(COMPONENTS):
                    tile[k, block, place, :] = values[k].astype(BF16)

    def product(sweep, blocks, chunk, chunks):
        slots = range(2 * chunks)
        xy = jnp.concatenate([density[sweep, 2 * chunk + i, 0:16, :] for i in slots], axis=1)
        zx = jnp.concatenate([density[sweep, 2 * chunk + i, 16:32, :] for i in slots], axis=1)
        xyz = jnp.concatenate([xy, zx], axis=0)
        place = pl.ds(pl.multiple_of(chunk * 256, 256), chunks * 256)

        def dot(left, k):
            right = jnp.concatenate([tile[k, block, place, :] for block in blocks], axis=1)
            return jnp.dot(left, right, preferred_element_type=F32)

        p_xx = dot(xy, 0)
        p_xy = dot(xy, 1)
        p_xz = dot(zx, 2)
        p_yy = dot(xy, 3)
        p_yz = dot(xyz, 4)
        p_zz = dot(zx, 5)
        return (
            p_xx[0:8] + p_xy[8:16] + p_xz[0:8],
            p_xy[0:8] + p_yy[8:16] + p_yz[16:24],
            p_xz[8:16] + p_yz[8:16] + p_zz[0:8],
        )

    def accumulate(sweep, blocks, sums, first):
        for part, block in enumerate(blocks):
            for i in range(3):
                value = sums[i][:, part * OWN : (part + 1) * OWN]
                if not first:
                    value = value + partial[sweep, block, i]
                partial[sweep, block, i] = value

    def send_partial(sweep, blocks):
        for block in blocks:
            if block < BLOCKS - 1:
                partial_copy(sweep, block).start()

    def total_of(sweep):
        total = [partial[sweep, BLOCKS - 1, i] for i in range(3)]
        for block in reversed(range(BLOCKS - 1)):
            partial_copy(sweep, block).wait_recv()
            for i in range(3):
                total[i] = total[i] + arrived[sweep, block, i]
        return total

    stiffness = stiffness_ref[pl.ds(half, 1), :]

    def next_density(sweep):
        total = total_of(sweep)
        send_density(sweep + 1, [trac[i] - stiffness * total[i] for i in range(3)])()

    brick_side(
        (
            nodal,
            connect,
            size_ref,
            shear_ref,
            bulk_ref,
            cohesion_ref,
            friction_ref,
            active_ref,
            brick_ref,
            face_ref,
        ),
        half,
        trac,
        fem,
    )
    start_density = send_density(0, [trac[i] for i in range(3)])
    widen(0)

    pl.semaphore_wait(barrier, SLOTS - 1 + 2 * (BLOCKS - 1))

    for slot in range(1, 2 * NEAR):
        place_copy(slot).start()
    for block in range(BLOCKS - 1):
        target_copy(block).start()
    for slot in reversed(range(2 * NEAR, SLOTS)):
        place_copy(slot).start()
    start_density()
    fem_copy().start()

    for slot in range(1, 2 * NEAR):
        place_copy(slot).wait_recv()

    for slot in range(1, 2 * NEAR):
        widen(slot)

    for pair in reversed(range(PAIRS)):
        for block in (2 * pair, 2 * pair + 1):
            if block < BLOCKS - 1:
                target_copy(block).wait_recv()

        @pl.loop(0, NEAR)
        def _(chunk):
            tile_piece(pair, chunk)

    for slot in range(2 * NEAR, SLOTS):
        place_copy(slot).wait_recv()

    @pl.loop(2 * NEAR, SLOTS, step=6)
    def _(slot):
        for i in range(6):
            widen(slot + i)

    for slot in range(1, SLOTS):
        density_copy(0, slot).wait_recv()

    for pair in range(PAIRS):

        @pl.loop(NEAR, CHUNKS, step=2)
        def _(chunk):
            tile_piece(pair, chunk)
            tile_piece(pair, chunk + 1)

        blocks = (2 * pair, 2 * pair + 1)
        accumulate(0, blocks, product(0, blocks, 0, CHUNKS), True)
        send_partial(0, blocks)

    next_density(0)

    @pl.loop(1, SWEEPS)
    def _(sweep):
        remote, near_pair = range(BLOCKS - 2), range(BLOCKS - 2, BLOCKS)
        for slot in range(1, 2 * EARLY):
            density_copy(sweep, slot).wait_recv()
        accumulate(sweep, remote, product(sweep, remote, 0, EARLY), True)
        for slot in range(2 * EARLY, SLOTS):
            density_copy(sweep, slot).wait_recv()
        for pair in range(PAIRS):
            blocks = (2 * pair, 2 * pair + 1)
            if pair < PAIRS - 1:
                sums = product(sweep, blocks, EARLY, CHUNKS - EARLY)
                accumulate(sweep, blocks, sums, False)
            else:
                accumulate(sweep, blocks, product(sweep, blocks, 0, CHUNKS), True)

            @pl.when(sweep == SWEEPS - 1)
            def _():
                for block in blocks:
                    beside_copy(block).start()

            send_partial(sweep, blocks)

        @pl.when(sweep < SWEEPS - 1)
        def _():
            next_density(sweep)

    for slot in range(1, SLOTS):
        place_copy(slot).wait_send()
    for block in range(BLOCKS - 1):
        target_copy(block).wait_send()
    fem_copy().wait()

    @pl.loop(0, SWEEPS)
    def _(sweep):
        for slot in range(1, SLOTS):
            density_copy(sweep, slot).wait_send()
        for block in range(BLOCKS - 1):
            partial_copy(sweep, block).wait_send()

    own_total = total_of(SWEEPS - 1)
    for block in range(BLOCKS):
        beside_copy(block).wait_send()
    other_total = [jnp.zeros((8, OWN), F32)] * 3
    for block in reversed(range(BLOCKS)):
        beside_copy(block).wait_recv()
        for i in range(3):
            other_total[i] = other_total[i] + beside[block, i]
    for i in range(3):
        own_out = fem[0, i] + RELAXATION * (own_total[i] - fem[0, i])
        other_out = fem[1, i] + RELAXATION * (other_total[i] - fem[1, i])
        low = jnp.where(half == 0, own_out, other_out)
        high = jnp.where(half == 0, other_out, own_out)
        out_ref[i] = jnp.concatenate([low, high], axis=1)


def on_device(
    nodal_disp,
    connect,
    brick_size,
    shear_modulus,
    bulk_modulus,
    cohesion,
    friction,
    active,
    patch_brick,
    patch_face,
    coords,
    radius,
    stiffness,
):
    batches = nodal_disp.shape[0]
    local_nodes = coords.shape[1]
    anywhere = pl.BlockSpec(memory_space=pl.ANY)
    vmem = pl.BlockSpec(memory_space=pltpu.VMEM)
    dma = pltpu.SemaphoreType.DMA
    by_brick = [
        values.reshape(-1, 128)
        for values in (brick_size, shear_modulus, bulk_modulus, cohesion, friction, active)
    ]
    by_node = [values.reshape(-1, OWN) for values in (patch_brick, patch_face)]
    inputs = (
        nodal_disp.transpose(1, 0, 2),
        connect,
        *by_brick,
        *by_node,
        coords,
        radius.reshape(-1, OWN),
        stiffness.reshape(-1, OWN),
    )
    relaxed = pl.pallas_call(
        kernel,
        out_shape=jax.ShapeDtypeStruct((3, batches, local_nodes), F32),
        in_specs=[anywhere] * len(inputs),
        out_specs=vmem,
        scratch_shapes=[
            *(pltpu.VMEM(values.shape, values.dtype) for values in inputs),
            pltpu.VMEM((8, OWN), F32),
            pltpu.VMEM((SLOTS, 8, OWN), F32),
            pltpu.VMEM((BLOCKS, 8, OWN), F32),
            pltpu.VMEM((5, SOURCES, 128), F32),
            pltpu.VMEM((COMPONENTS, BLOCKS, SOURCES, 128), BF16),
            pltpu.VMEM((SWEEPS, SLOTS, 32, OWN), BF16),
            pltpu.VMEM((SWEEPS, BLOCKS, 3, 8, OWN), F32),
            pltpu.VMEM((SWEEPS, BLOCKS, 3, 8, OWN), F32),
            pltpu.VMEM((3, 8, OWN), F32),
            pltpu.VMEM((2, 3, 8, OWN), F32),
            pltpu.VMEM((BLOCKS, 3, 8, OWN), F32),
            pltpu.VMEM((32, 5 * 128), BF16),
            dma((len(inputs),)),
            dma((SLOTS,)),
            dma((SLOTS,)),
            dma((BLOCKS,)),
            dma((BLOCKS,)),
            dma((SWEEPS, SLOTS)),
            dma((SWEEPS, SLOTS)),
            dma((SWEEPS, BLOCKS)),
            dma((SWEEPS, BLOCKS)),
            dma((BLOCKS,)),
            dma((BLOCKS,)),
            dma,
            dma,
        ],
        compiler_params=pltpu.CompilerParams(
            collective_id=0, has_side_effects=True, vmem_limit_bytes=60 * 2**20
        ),
    )(
        *inputs
    )
    return relaxed.transpose(1, 0, 2)


def solution(mesh):
    split = ("blk", "rows")
    return jax.shard_map(
        on_device,
        mesh=mesh,
        in_specs=(
            P(None, None, split),
            P(None, split),
            P(split),
            P(split),
            P(split),
            P(split),
            P(split),
            P(split),
            P(split),
            P(split),
            P(None, split),
            P(split),
            P(split),
        ),
        out_specs=P(None, None, split),
        check_vma=False,
    )
```
